256 devices in a mesh: lat: 8 (over z), lon: 16 (over y, x_lo, core), grp: 2 (over x_hi).
Axes of the slice: x: 4 (x_hi: 2, x_lo: 2; x = x_hi * 2 + x_lo), y: 4, z: 8, core: 2. Of those that a mesh axis runs over, the one named last changes fastest.
Arguments:
- columns: float32 [2, 278, 128, 2048], P('grp', None, 'lat', 'lon'), may hold values from -6 to 6
- east_courant: float32 [128, 2048], P('lat', 'lon'), may hold values from 0.05 to 0.45
- north_courant: float32 [128, 2048], P('lat', 'lon'), may hold values from 0.05 to 0.45
- assign: int32 [8, 16, 16], replicated, may hold values from 0 to 255, as said below
- block_cost: int32 [8, 16, 16], replicated, may hold values from 1 to 128, as said below
- w_in: bfloat16 [556, 384], replicated, may hold values from -0.25 to 0.25
- w_mid: bfloat16 [384, 384], replicated, may hold values from -0.3125 to 0.3125
- w_out: bfloat16 [384, 368], replicated, may hold values from -0.3125 to 0.3125
- energy: float32 [368], replicated, may hold values from -4 to 4
Outputs:
- new_columns: float32 [2, 278, 128, 2048], P('grp', None, 'lat', 'lon')
- gradients: float32 [502272], P('grp')
The draws below stay inside these ranges and needn't reach their ends.
Inputs may be any that keep to these rules, and one draw needn't show every extreme that they name: For each band b, assign[b] holds every number 0 to 255 once. The blocks of one device that go to one physics device of its band number 0 or exactly 1. `block_cost`: every band has a block with all 128 columns live.
All inputs are finite; a program needn't handle non-finite values.
Results may differ from the reference program's by a relative error of at most 0.0019.
Values may be sent and summed in bfloat16 or wider, within the bound.
No kernel may reach another device: no remote copies, remote signals or barrier semaphores. Data moves between devices by JAX's collectives and lax.ppermute only.
A program may use at most 128 MiB of HBM per device.

```python
import math
import jax
import jax.numpy as jnp
from jax import lax

IN = 556
HID = 384
OUT = 368
HALF = 278
CLAT = 16
CLON = 128
PAIR = 1
NLAT = 128
NLON = 2048
P_SIZE = 502272
N_LAT = 8
N_LON = 16


def draw_assign(key, part):
    key = jax.random.fold_in(key, 11)
    keys = jax.random.split(key, 4)

    def shuffle_rows(sub_key):
        return jax.random.permutation(sub_key, CLAT)

    def shuffle_lanes(sub_key):
        return jax.random.permutation(sub_key, N_LON)
    local_order = jax.vmap(shuffle_rows)(jax.random.split(keys[0], N_LAT * N_LON)).reshape(N_LAT, N_LON, CLAT)
    group_ids = local_order // PAIR
    lane_order = jax.vmap(shuffle_lanes)(jax.random.split(keys[1], N_LAT))
    offset = jax.random.randint(keys[2], (N_LAT, 1, 1), 0, N_LON)
    source_ids = jnp.arange(N_LON, dtype=jnp.int32)[None, :, None]
    position = (source_ids + group_ids + offset) % N_LON
    lane_ids = jnp.arange(N_LON, dtype=jnp.int32)
    dest_ids = jnp.sum(jnp.where(position[..., None] == lane_ids, lane_order[:, None, None, :], 0), axis=-1)
    slot_order = jax.vmap(shuffle_rows)(jax.random.split(keys[3], N_LAT * N_LON)).reshape(N_LAT, N_LON, CLAT)
    dest_match = (dest_ids[..., None] == lane_ids)[..., None]
    row_pick = jnp.sum(jnp.where(dest_match, slot_order[:, None, None, :, :], 0), axis=3)
    slot_ids = jnp.sum(jnp.where(local_order[..., None] == jnp.arange(CLAT, dtype=jnp.int32), row_pick, 0), axis=-1)
    return (dest_ids * CLAT + slot_ids).astype(jnp.int32)


def draw_block_cost(key, part):
    key = jax.random.fold_in(key, 23)
    keys = jax.random.split(key, 3)
    level = jax.random.randint(keys[0], (N_LAT, N_LON, 1), 1, 5)
    ceiling = level * CLON // 4 + 1
    drawn = jax.random.randint(keys[1], (N_LAT, N_LON, CLAT), 1, ceiling)
    full_at = jax.random.randint(keys[2], (N_LAT, 1), 0, N_LON * CLAT)
    flat_cost = drawn.reshape(N_LAT, N_LON * CLAT)
    flat_cost = jnp.where(jnp.arange(N_LON * CLAT, dtype=jnp.int32)[None, :] == full_at, CLON, flat_cost)
    return flat_cost.reshape(N_LAT, N_LON, CLAT).astype(jnp.int32)


def level_of(rng, dims, cuts, low, high):
    gain, own = 1.0, jax.random.fold_in(rng, 6)
    for axis_at, shards_of in cuts:
        steps = jnp.exp(jax.random.uniform(jax.random.fold_in(own, axis_at), (shards_of,), jnp.float32, low / len(cuts), high / len(cuts)))
        gain = gain * jnp.repeat(steps, dims[axis_at] // shards_of).reshape([-1 if axis == axis_at else 1 for axis in range(len(dims))])
    return gain


def scatter_about(own_key, dims, scale, most, cuts=(), kind=jnp.bfloat16):
    factor_of = level_of(own_key, dims, cuts, -0.22, 0.18) if cuts else 1.0
    values = jax.random.normal(own_key, dims, jnp.float32) * scale * factor_of
    return jnp.minimum(jnp.maximum(values, -most), most).astype(kind)


def setup_inputs(seed: int = 0) -> dict:
    seeds = jax.random.split(jax.random.key(seed), 10)
    return {
        "columns": scatter_about(seeds[0], (2, HALF, NLAT, NLON), 1.0, 6.0, ((0, 2), (2, 8), (3, 16)), jnp.float32),
        "east_courant": jnp.clip(0.05 + 0.39999999 * jax.random.uniform(seeds[1], (NLAT, NLON), jnp.float32) ** level_of(seeds[1], (NLAT, NLON), ((0, 8), (1, 16)), -0.2, 0.2), 0.05, 0.45),
        "north_courant": jnp.clip(0.05 + 0.39999999 * jax.random.uniform(seeds[2], (NLAT, NLON), jnp.float32) ** level_of(seeds[2], (NLAT, NLON), ((0, 8), (1, 16)), -0.2, 0.2), 0.05, 0.45),
        "assign": draw_assign(jax.random.fold_in(seeds[9], 71), 0),
        "block_cost": draw_block_cost(jax.random.fold_in(seeds[9], 71), 0),
        "w_in": scatter_about(seeds[5], (IN, HID), IN ** -0.5, 0.25),
        "w_mid": scatter_about(seeds[6], (HID, HID), HID ** -0.5, 0.3125),
        "w_out": scatter_about(seeds[7], (HID, OUT), HID ** -0.5, 0.3125),
        "energy": scatter_about(seeds[8], (OUT,), 1.0, 4.0, (), jnp.float32),
    }


step_weight = 0.5

def upwind(grid_field, east_courant, north_courant):
    flux_x = east_courant[None] * grid_field
    flux_y = north_courant[None] * grid_field
    row_ids = lax.broadcasted_iota(jnp.int32, flux_y.shape, 1)
    flux_y = jnp.where(row_ids == flux_y.shape[1] - 1, 0.0, flux_y)
    inflow_x = jnp.roll(flux_x, 1, axis=2)
    inflow_y = jnp.concatenate([jnp.zeros_like(flux_y[:, :1]), flux_y[:, :-1]], axis=1)
    return grid_field - flux_x + inflow_x - flux_y + inflow_y

def silu_slope(pre_act):
    sigmoid_value = jax.nn.sigmoid(pre_act)
    return sigmoid_value * (1.0 + pre_act * (1.0 - sigmoid_value))

def network(inputs, live_mask, w_in, w_mid, w_out, energy, loss_norm):
    pre_one = jnp.dot(w_in.T, inputs, preferred_element_type=jnp.float32)
    hidden_one = jax.nn.silu(pre_one).astype(jnp.bfloat16)
    pre_two = jnp.dot(w_mid.T, hidden_one, preferred_element_type=jnp.float32)
    hidden_two = jax.nn.silu(pre_two).astype(jnp.bfloat16)
    result = jnp.dot(w_out.T, hidden_two, preferred_element_type=jnp.float32).astype(jnp.bfloat16)
    column_energy = lax.optimization_barrier(jnp.sum(energy[:, None] * result.astype(jnp.float32), axis=0)) / math.sqrt(energy.shape[0])
    g_result = (energy[:, None] * (live_mask * column_energy * loss_norm)[None, :]).astype(jnp.bfloat16)
    d_out = jnp.dot(hidden_two, g_result.T, preferred_element_type=jnp.float32)
    g_two = (jnp.dot(w_out, g_result, preferred_element_type=jnp.float32) * silu_slope(pre_two)).astype(jnp.bfloat16)
    d_mid = jnp.dot(hidden_one, g_two.T, preferred_element_type=jnp.float32)
    g_one = (jnp.dot(w_mid, g_two, preferred_element_type=jnp.float32) * silu_slope(pre_one)).astype(jnp.bfloat16)
    d_in = jnp.dot(inputs, g_one.T, preferred_element_type=jnp.float32)
    return (result, jnp.concatenate([d_in.reshape(-1), d_mid.reshape(-1), d_out.reshape(-1)]))

def reference(columns, east_courant, north_courant, assign, block_cost, w_in, w_mid, w_out, energy):
    per_band = N_LON * CLAT
    state_field = upwind(columns[0], east_courant, north_courant)
    state_field = upwind(state_field, east_courant, north_courant)

    def to_blocks(grid_field):
        feature_count = grid_field.shape[0]
        shaped = grid_field.reshape(feature_count, N_LAT, CLAT, N_LON, CLON)
        return shaped.transpose(0, 1, 3, 2, 4).reshape(feature_count, N_LAT, per_band, CLON)

    def to_grid(blocks):
        feature_count = blocks.shape[0]
        shaped = blocks.reshape(feature_count, N_LAT, N_LON, CLAT, CLON)
        return shaped.transpose(0, 1, 3, 2, 4).reshape(feature_count, NLAT, NLON)
    targets = assign.reshape(N_LAT, per_band).astype(jnp.int32)
    band_rows = jnp.arange(N_LAT, dtype=jnp.int32)[:, None]
    home_ids = jnp.broadcast_to(jnp.arange(per_band, dtype=jnp.int32)[None, :], targets.shape)
    sender = jnp.zeros_like(targets).at[band_rows, targets].set(home_ids)
    home_cost = block_cost.reshape(N_LAT, per_band)
    slot_cost = jnp.take_along_axis(home_cost, sender, axis=1)
    column_ids = jnp.arange(CLON, dtype=jnp.int32)
    slot_live = (column_ids[None, None, :] < slot_cost[:, :, None]).astype(jnp.float32)
    home_live = (column_ids[None, None, :] < home_cost[:, :, None]).astype(jnp.float32)
    home_state = to_blocks(state_field.astype(jnp.bfloat16))
    slot_state = jnp.take_along_axis(home_state, sender[None, :, :, None], axis=2)
    memory = to_blocks(columns[1])
    inputs = jnp.concatenate([slot_state, memory.astype(jnp.bfloat16)], axis=0)
    loss_norm = 1.0 / math.sqrt(NLAT * NLON)

    def one_band(carry, band_data):
        band_inputs, band_live = band_data
        result, gradient = network(band_inputs.reshape(IN, per_band * CLON), band_live.reshape(-1), w_in, w_mid, w_out, energy, loss_norm)
        return (carry + gradient, result)
    gradient, results = lax.scan(one_band, jnp.zeros((P_SIZE,), jnp.float32), (jnp.moveaxis(inputs, 1, 0), slot_live))
    results = jnp.moveaxis(results.reshape(N_LAT, OUT, per_band, CLON), 0, 1)
    home_tend = jnp.take_along_axis(results[:HALF], targets[None, :, :, None], axis=2)
    new_state = state_field + step_weight * to_grid(home_live[None]) * to_grid(home_tend).astype(jnp.float32)
    new_memory = to_grid(jnp.where(slot_live[None] > 0, results[OUT - HALF:].astype(jnp.float32), memory))
    return (jnp.stack([new_state, new_memory]), gradient)
```

```python
import functools
import math

import jax
import jax.numpy as jnp
from jax import lax
from jax.experimental import pallas as pl
from jax.experimental.pallas import tpu as pltpu
from jax.sharding import Mesh, PartitionSpec as P

f32 = jnp.float32
bf16 = jnp.bfloat16

FEAT = 278
FPAD = 288
PACK = 144
ROWS = 16
COLS = 128
HID = 384
OUT = 368
FLAT = FEAT * ROWS
MINE = ROWS * COLS // 2
LON = ("y", "x", "core")
VMEM_LIMIT = 50 * 1024 * 1024

NT = (((1,), (1,)), ((), ()))
TN = (((0,), (0,)), ((), ()))

A_ROWS = 680
B_ROWS = 288
OWNERS = 128
A_PIECE = 16
B_PIECE = 8
PIECE = A_PIECE + B_PIECE


def vmem_call(kernel, outs, scratch, n_smem, n_vmem, flops, size, name):
    return pl.pallas_call(
        kernel,
        out_shape=outs,
        in_specs=[pl.BlockSpec(memory_space=pltpu.SMEM)] * n_smem
        + [pl.BlockSpec(memory_space=pltpu.VMEM)] * n_vmem,
        out_specs=jax.tree.map(lambda _: pl.BlockSpec(memory_space=pltpu.VMEM), outs),
        scratch_shapes=scratch,
        compiler_params=pltpu.CompilerParams(vmem_limit_bytes=VMEM_LIMIT),
        cost_estimate=pl.CostEstimate(flops=flops, bytes_accessed=size, transcendentals=0),
        name=name,
    )


def lane_ids(shape):
    return lax.broadcasted_iota(jnp.int32, shape, len(shape) - 1)


def row_ids(shape):
    return lax.broadcasted_iota(jnp.int32, shape, len(shape) - 2)


def chunks():
    full = FEAT // 8
    return full, FEAT - full * 8


def coefficients(east, north, flags_ref):
    dyn = flags_ref[0]
    not_top = flags_ref[1]
    rows = row_ids(north.shape)
    north = jnp.where(rows == ROWS - 1, north * not_top, north) * dyn
    east = east * dyn
    keep = 1.0 - east - north
    west = jnp.where(lane_ids(east.shape) == 0, 0.0, pltpu.roll(east, 1, 1))
    south = jnp.where(rows == 0, 0.0, pltpu.roll(north, 1, 0))
    return east, north, keep, west, south


def step(q, keep, west, south):
    shaped = q.reshape(-1, ROWS, COLS)
    out = (
        keep[None] * shaped
        + west[None] * pltpu.roll(shaped, 1, 2)
        + south[None] * pltpu.roll(shaped, 1, 1)
    )
    return out


def rim_kernel(flags_ref, x_ref, east_ref, north_ref, rim_ref, north_out_ref):
    east, north, keep, west, south = coefficients(east_ref[...], north_ref[...], flags_ref)
    pick_rows = row_ids((16, COLS))
    last = lane_ids((16, COLS)) == COLS - 1

    def pick(k):
        return jnp.where(jnp.logical_and(pick_rows == k, last), 1.0, 0.0).astype(bf16)

    def piece(start, count):
        q = x_ref[pl.ds(start * ROWS, count * ROWS), :]
        shaped = q.reshape(count, ROWS, COLS)
        after = step(q, keep, west, south)
        flux_one = (east[None] * shaped).reshape(count * ROWS, COLS).astype(bf16)
        flux_two = (east[None] * after).reshape(count * ROWS, COLS).astype(bf16)
        flux_up = (north[None] * shaped).reshape(count * ROWS, COLS).astype(bf16)
        out = lax.dot_general(pick(0), flux_one, NT, preferred_element_type=f32)
        out += lax.dot_general(pick(1), flux_two, NT, preferred_element_type=f32)
        out += lax.dot_general(pick(2), flux_up, NT, preferred_element_type=f32)
        corner = jnp.broadcast_to(east[0:1, COLS - 1 : COLS], out.shape)
        return jnp.where(row_ids(out.shape) == 3, corner, out).astype(bf16)

    full, rest = chunks()

    def body(i, carry):
        rim_ref[:, pl.ds(pl.multiple_of(i * 128, 128), 128)] = piece(i * 8, 8)
        return carry

    lax.fori_loop(0, full, body, 0, unroll=2)
    rim_ref[:, full * 128 : full * 128 + rest * ROWS] = piece(full * 8, rest)
    rim_ref[:, full * 128 + rest * ROWS :] = jnp.zeros(
        (16, rim_ref.shape[1] - full * 128 - rest * ROWS), bf16
    )
    q_top = x_ref[pl.ds(ROWS - 1, FEAT, stride=ROWS), :]
    q_under = x_ref[pl.ds(ROWS - 2, FEAT, stride=ROWS), :]
    top = slice(ROWS - 1, ROWS)
    after_top = (
        keep[top] * q_top + west[top] * pltpu.roll(q_top, 1, 1) + south[top] * q_under
    )
    north_out_ref[0:FEAT, :] = (north[top] * q_top).astype(bf16)
    north_out_ref[FPAD : FPAD + FEAT, :] = (north[top] * after_top).astype(bf16)
    pad = jnp.broadcast_to(north[top], (FPAD - FEAT, COLS)).astype(bf16)
    north_out_ref[FEAT:FPAD, :] = pad
    north_out_ref[FPAD + FEAT :, :] = pad


def transport_kernel(
    table_ref, flags_ref, x_ref, east_ref, north_ref, rim_ref, south_ref, corner_ref,
    field_ref, own_ref, send_ref, mid_ref, row_ref,
):
    east, north, keep, west, south = coefficients(east_ref[...], north_ref[...], flags_ref)
    full, rest = chunks()
    row16 = row_ids((16, COLS))
    lane16 = lane_ids((16, COLS))

    def put(k):
        return jnp.where(jnp.logical_and(row16 == k, lane16 == 0), 1.0, 0.0).astype(bf16)

    def column(values, k):
        return lax.dot_general(values, put(k), TN, preferred_element_type=f32)

    def first(start, count, lanes):
        q = x_ref[pl.ds(start * ROWS, count * ROWS), :]
        rim = rim_ref[:, lanes]
        inflow = column(rim, 0)[: count * ROWS]
        after = step(q, keep, west, south).reshape(count * ROWS, COLS) + inflow
        mid_ref[pl.ds(start * ROWS, count * ROWS), :] = after

    def first_body(i, carry):
        first(i * 8, 8, pl.ds(pl.multiple_of(i * 128, 128), 128))
        return carry

    lax.fori_loop(0, full, first_body, 0, unroll=2)
    first(full * 8, rest, slice(full * 128, full * 128 + 128))
    row0 = pl.ds(0, FEAT, stride=ROWS)
    mid_ref[row0, :] = mid_ref[row0, :] + south_ref[0:FEAT, :].astype(f32)

    def second(start, count, lanes):
        q = mid_ref[pl.ds(start * ROWS, count * ROWS), :]
        rim = rim_ref[:, lanes].astype(f32)
        corner = corner_ref[:, lanes]
        moved = pltpu.roll(corner.astype(f32), 128 - (ROWS - 1), 1)
        moved = jnp.where(lane_ids((1, 128)) % ROWS == 0, moved[2:3, :] * rim[3:4, :], 0.0)
        inflow_row = (rim[1:2, :] + moved).astype(bf16)
        values = jnp.broadcast_to(inflow_row, (16, 128))
        inflow = column(values, 0)[: count * ROWS]
        after = step(q, keep, west, south).reshape(count * ROWS, COLS) + inflow
        field_ref[pl.ds(start * ROWS, count * ROWS), :] = after
        row_ref[pl.ds(start * ROWS, count * ROWS), :] = column(corner, 0)[: count * ROWS]

    def second_body(i, carry):
        second(i * 8, 8, pl.ds(pl.multiple_of(i * 128, 128), 128))
        return carry

    lax.fori_loop(0, full, second_body, 0, unroll=2)
    second(full * 8, rest, slice(full * 128, full * 128 + 128))
    south_courant = south_ref[FEAT : FEAT + 1, 0:1].astype(f32)
    extra = row_ref[pl.ds(ROWS - 1, FEAT, stride=ROWS), :] * south_courant
    field_ref[row0, :] = (
        field_ref[row0, :] + south_ref[FPAD : FPAD + FEAT, :].astype(f32) + extra
    )

    turn = table_ref[2, 0]
    to_slot = table_ref[2, 1]
    low = lane_ids((PACK, COLS)) < COLS // 2
    zeros = jnp.zeros((FPAD - FEAT, COLS), f32)

    def block(r):
        rows = pl.ds(table_ref[0, r], FEAT, stride=ROWS)
        value = jnp.concatenate([field_ref[rows, :], zeros], axis=0)
        return pltpu.roll(value, turn, 1)

    def half(value):
        return pltpu.roll(value, COLS // 2, 1)

    def pair_body(i, carry):
        kept = []
        for side in range(2):
            r = 2 * i + side
            value = block(r)
            other = half(value)
            packed = jnp.where(low, other[:PACK], value[PACK:])
            send_ref[2 * r + to_slot] = packed.astype(bf16)
            send_ref[2 * r + 1 - to_slot] = jnp.zeros((PACK, COLS), bf16)
            kept.append(value if side == 0 else other)
        low_full = lane_ids((FPAD, COLS)) < COLS // 2
        own_ref[:, pl.ds(pl.multiple_of(i * COLS, COLS), COLS)] = jnp.where(
            low_full, kept[0], kept[1]
        ).astype(bf16)
        return carry

    lax.fori_loop(0, ROWS // 2, pair_body, 0)


def swap_halves(value):
    return pltpu.roll(value, COLS // 2, 1)


def forward_kernel(
    table_ref, own_ref, recv_ref, w_one_ref, w_two_ref, w_three_ref, gain_ref,
    inputs_ref, hidden_ref, g_two_ref, slope_ref, own_out_ref, send_ref, vec_ref,
):
    from_slot = table_ref[2, 1]
    offset = table_ref[2, 2]
    low = lane_ids((PACK, COLS)) < COLS // 2
    gain = gain_ref[...]
    loss_norm = 1.0 / math.sqrt(ROWS * 8 * COLS * ROWS)
    energy_norm = 1.0 / math.sqrt(OUT)
    tile = 2 * COLS
    vec_ref[...] = jnp.zeros(vec_ref.shape, f32)

    def tile_body(t, carry):
        lanes = pl.ds(pl.multiple_of(t * tile, tile), tile)
        live_parts = []
        for g in range(2):
            i = 2 * t + g
            group = pl.ds(pl.multiple_of(i * COLS, COLS), COLS)
            first = recv_ref[4 * i + from_slot].astype(f32)
            second = recv_ref[4 * i + 2 + from_slot].astype(f32)
            inputs_ref[0:FPAD, group] = own_ref[:, group]
            inputs_ref[FPAD : FPAD + PACK, group] = jnp.where(
                low, first, swap_halves(second)
            ).astype(bf16)
            inputs_ref[FPAD + PACK :, group] = jnp.where(
                low, swap_halves(first), second
            ).astype(bf16)
            lane = lane_ids((1, COLS))
            column = lane % (COLS // 2) + offset
            cost = jnp.where(lane < COLS // 2, table_ref[1, 2 * i], table_ref[1, 2 * i + 1])
            live_parts.append(jnp.where(column < cost, 1.0, 0.0))
        live = jnp.concatenate(live_parts, axis=1)
        inputs = inputs_ref[:, lanes]
        pre_one = jnp.dot(w_one_ref[...], inputs, preferred_element_type=f32)
        sig = 1.0 / (1.0 + jnp.exp(-pre_one))
        hidden_one = (pre_one * sig).astype(bf16)
        slope_ref[:, lanes] = sig * (1.0 + pre_one * (1.0 - sig))
        hidden_ref[:, lanes] = hidden_one
        pre_two = jnp.dot(w_two_ref[...], hidden_one, preferred_element_type=f32)
        sig = 1.0 / (1.0 + jnp.exp(-pre_two))
        hidden_two = (pre_two * sig).astype(bf16)
        slope_two = sig * (1.0 + pre_two * (1.0 - sig))
        result = jnp.dot(w_three_ref[...], hidden_two, preferred_element_type=f32).astype(bf16)
        own_out_ref[:, lanes] = result[:FPAD]
        to_send = result[FPAD:].astype(f32)
        for g in range(2):
            i = 2 * t + g
            part = to_send[:, g * COLS : (g + 1) * COLS]
            other = swap_halves(part)
            zeros = jnp.zeros((PACK, COLS), bf16)
            send_ref[4 * i + from_slot] = jnp.where(low, part[:PACK], other[PACK:]).astype(bf16)
            send_ref[4 * i + 2 + from_slot] = jnp.where(
                low, other[:PACK], part[PACK:]
            ).astype(bf16)
            send_ref[4 * i + 1 - from_slot] = zeros
            send_ref[4 * i + 3 - from_slot] = zeros
        energy = jnp.sum(gain * hidden_two.astype(f32), axis=0, keepdims=True) * energy_norm
        weight = live * energy * loss_norm
        g_two_ref[:, lanes] = (gain * weight * slope_two).astype(bf16)
        high = weight.astype(bf16)
        left = weight - high.astype(f32)
        mid = left.astype(bf16)
        low_part = (left - mid.astype(f32)).astype(bf16)
        rows = row_ids((16, tile))
        stacked = jnp.where(
            rows == 0,
            high.astype(f32),
            jnp.where(rows == 1, mid.astype(f32), jnp.where(rows == 2, low_part.astype(f32), 0.0)),
        ).astype(bf16)
        vec_ref[...] += lax.dot_general(stacked, hidden_two, NT, preferred_element_type=f32)
        return carry

    lax.fori_loop(0, MINE // tile, tile_body, 0)


def backward_kernel(
    table_ref, inputs_ref, hidden_ref, g_two_ref, slope_ref, w_mid_ref, vec_ref,
    grad_ref, g_one_ref, d_in_ref,
):
    state_first = table_ref[2, 3]
    tile = 2 * COLS

    def tile_body(t, carry):
        lanes = pl.ds(pl.multiple_of(t * tile, tile), tile)
        back = jnp.dot(w_mid_ref[...], g_two_ref[:, lanes], preferred_element_type=f32)
        g_one_ref[:, lanes] = (back * slope_ref[:, lanes]).astype(bf16)
        return carry

    lax.fori_loop(0, MINE // tile, tile_body, 0)
    d_mid = lax.dot_general(hidden_ref[...], g_two_ref[...], NT, preferred_element_type=f32)
    g_one = g_one_ref[...]
    own_at = pl.multiple_of((1 - state_first) * FPAD, 8)
    recv_at = pl.multiple_of(state_first * FPAD, 8)
    d_in_ref[pl.ds(own_at, FPAD), :] = lax.dot_general(
        inputs_ref[:FPAD, :], g_one, NT, preferred_element_type=f32
    )
    d_in_ref[pl.ds(recv_at, FPAD), :] = lax.dot_general(
        inputs_ref[FPAD:, :], g_one, NT, preferred_element_type=f32
    )
    d_in = d_in_ref[...]

    def put_a(row, value):
        grad_ref[row // A_PIECE, row % A_PIECE : row % A_PIECE + 8, :] = value

    def put_b(row, value):
        grad_ref[row // B_PIECE, A_PIECE:PIECE, :] = value

    for l in range(3):
        lanes = slice(l * 128, (l + 1) * 128)
        for k in range(2 * FPAD // 8):
            put_a(l * A_ROWS + k * 8, d_in[k * 8 : k * 8 + 8, lanes])
        for k in range((A_ROWS - 2 * FPAD) // 8):
            put_a(l * A_ROWS + 2 * FPAD + k * 8, d_mid[k * 8 : k * 8 + 8, lanes])
        for k in range(B_ROWS // 8):
            put_b(l * B_ROWS + k * 8, d_mid[96 + k * 8 : 96 + k * 8 + 8, lanes])
    zeros = jnp.zeros((8, 128), f32)
    for row in range(3 * A_ROWS, OWNERS * A_PIECE, 8):
        put_a(row, zeros)
    vec = jnp.sum(vec_ref[...], axis=0, keepdims=True)
    for l in range(3):
        put_b(3 * B_ROWS + l * 8, jnp.broadcast_to(vec[:, l * 128 : (l + 1) * 128], (8, 128)))
    for row in range(3 * B_ROWS + 24, OWNERS * B_PIECE, 8):
        put_b(row, zeros)


def final_kernel(table_ref, scale_ref, field_ref, own_ref, recv_ref, out_ref):
    turn = table_ref[2, 0]
    from_slot = table_ref[2, 1]
    keep_scale = scale_ref[2]
    new_scale = scale_ref[3]
    low = lane_ids((PACK, COLS)) < COLS // 2
    low_full = lane_ids((FPAD, COLS)) < COLS // 2

    def pair_body(i, carry):
        pair = own_ref[:, pl.ds(pl.multiple_of(i * COLS, COLS), COLS)].astype(f32)
        for side in range(2):
            r = 2 * i + side
            chunk = recv_ref[2 * r + from_slot].astype(f32)
            theirs = jnp.concatenate([swap_halves(chunk), chunk], axis=0)
            mine = pair if side == 0 else swap_halves(pair)
            tend = pltpu.roll(jnp.where(low_full, mine, theirs), turn, 1)[:FEAT]
            rows = pl.ds(table_ref[0, r], FEAT, stride=ROWS)
            old = field_ref[rows, :]
            live = lane_ids((FEAT, COLS)) < table_ref[1, r]
            out_ref[rows, :] = jnp.where(live, keep_scale * old + new_scale * tend, old)
        return carry

    lax.fori_loop(0, ROWS // 2, pair_body, 0)


def shape(dims, dtype):
    return jax.ShapeDtypeStruct(dims, dtype)


def swap(value, axis):
    return lax.ppermute(value, axis, [(0, 1), (1, 0)])


def on_device(columns, east_courant, north_courant, assign, block_cost, w_in, w_mid, w_out, energy):
    band = lax.axis_index("lat")
    bands = lax.axis_size("lat")
    lon = lax.axis_index(LON)
    lons = lax.axis_size(LON)
    grp = lax.axis_index("grp")
    is_physics = grp == 1
    stored = columns.reshape(FLAT, COLS)

    dyn = (1 - grp).astype(f32)
    flags = jnp.stack(
        [dyn, (band != bands - 1).astype(f32), jnp.where(is_physics, 0.0, 1.0), jnp.where(is_physics, 1.0, 0.5)]
    )
    rim, north_out = vmem_call(
        rim_kernel,
        [shape((16, 35 * 128), bf16), shape((2 * FPAD, COLS), bf16)],
        [],
        1,
        3,
        10**8,
        3 * 10**6,
        "rim",
    )(flags, stored, east_courant, north_courant)
    from_west = lax.ppermute(rim, LON, [(i, (i + 1) % lons) for i in range(lons)])
    from_south = lax.ppermute(north_out, "lat", [(i, i + 1) for i in range(bands - 1)])
    from_corner = lax.ppermute(
        rim,
        ("lat",) + LON,
        [(b * lons + i, (b + 1) * lons + (i + 1) % lons) for b in range(bands - 1) for i in range(lons)],
    )

    targets = lax.dynamic_index_in_dim(assign, band, 0, keepdims=False)
    costs = lax.dynamic_index_in_dim(block_cost, band, 0, keepdims=False)
    owner = targets // ROWS
    ids = lax.broadcasted_iota(jnp.int32, (ROWS, ROWS), 0)
    ks = lax.broadcasted_iota(jnp.int32, (ROWS, ROWS), 1)
    here_owner = lax.dynamic_index_in_dim(owner, lon, 0, keepdims=True)
    here_cost = lax.dynamic_index_in_dim(costs, lon, 0, keepdims=True)
    match = jnp.where(is_physics, owner == lon, here_owner == ids)
    row_of = jnp.sum(jnp.where(match, jnp.where(is_physics, targets % ROWS, ks), 0), axis=1)
    cost_of = jnp.sum(jnp.where(match, jnp.where(is_physics, costs, here_cost), 0), axis=1)
    half = COLS // 2
    facts = jnp.stack([grp * half, 1 - grp, grp * half, 1 - grp]).astype(jnp.int32)
    table = jnp.stack([row_of, cost_of, jnp.pad(facts, (0, ROWS - 4))]).astype(jnp.int32)

    def halves(a, b, axis):
        first = jnp.where(is_physics, b, a)
        second = jnp.where(is_physics, a, b)
        pad = [(0, 0), (0, 0)]
        pad[axis] = (0, FPAD - FEAT)
        return jnp.concatenate([jnp.pad(first, pad), jnp.pad(second, pad)], axis=axis)

    w_in_t = w_in.T
    w_one = halves(w_in_t[:, :FEAT], w_in_t[:, FEAT:], 1)
    w_out_t = w_out.T
    w_three = halves(w_out_t[:FEAT], w_out_t[OUT - FEAT :], 0)
    gain = jnp.sum(w_out.astype(f32) * energy[None, :], axis=1, keepdims=True)

    field, own, send = vmem_call(
        transport_kernel,
        [shape((FLAT, COLS), f32), shape((FPAD, MINE), bf16), shape((2 * ROWS, PACK, COLS), bf16)],
        [pltpu.VMEM((FLAT, COLS), f32), pltpu.VMEM((FLAT, COLS), f32)],
        2,
        6,
        10**8,
        6 * 10**6,
        "transport",
    )(table, flags, stored, east_courant, north_courant, from_west, from_south, from_corner)
    recv = lax.all_to_all(send, LON + ("grp",), 0, 0, tiled=True)
    inputs, hidden, g_two, slope, own_out, send_back, vec = vmem_call(
        forward_kernel,
        [
            shape((2 * FPAD, MINE), bf16),
            shape((HID, MINE), bf16),
            shape((HID, MINE), bf16),
            shape((HID, MINE), f32),
            shape((FPAD, MINE), bf16),
            shape((2 * ROWS, PACK, COLS), bf16),
            shape((16, HID), f32),
        ],
        [],
        1,
        6,
        2 * MINE * HID * (4 * FPAD + HID),
        8 * 10**6,
        "forward",
    )(table, own, recv, w_one, w_mid.T, w_three, gain)
    back = lax.all_to_all(send_back, LON + ("grp",), 0, 0, tiled=True)
    grad = vmem_call(
        backward_kernel,
        [shape((OWNERS, PIECE, 128), f32)],
        [pltpu.VMEM((HID, MINE), bf16), pltpu.VMEM((2 * FPAD, HID), f32)],
        1,
        6,
        2 * MINE * HID * (2 * FPAD + 2 * HID),
        6 * 10**6,
        "backward",
    )(table, inputs, hidden, g_two, slope, w_mid, vec)[0]

    for axis in ("core", "x"):
        pieces = grad.shape[0] // 2
        at = lax.axis_index(axis)
        keep = lax.dynamic_slice_in_dim(grad, at * pieces, pieces)
        other = lax.dynamic_slice_in_dim(grad, (1 - at) * pieces, pieces)
        grad = keep + swap(other, axis)
    ring = ("lat", "y")
    members = bands * lax.axis_size("y")
    grad = jnp.sum(lax.all_to_all(grad, ring, 0, 0, tiled=True), axis=0)
    grad = grad + swap(grad, "grp")
    piece = jnp.where(
        is_physics, jnp.pad(grad[A_PIECE:], ((0, A_PIECE - B_PIECE), (0, 0))), grad[:A_PIECE]
    )
    piece = lax.all_to_all(
        jnp.broadcast_to(piece[None], (members,) + piece.shape), ring, 0, 0, tiled=True
    )
    for axis in ("x", "core"):
        other = swap(piece, axis)
        at_zero = lax.axis_index(axis) == 0
        piece = jnp.concatenate(
            [jnp.where(at_zero, piece, other), jnp.where(at_zero, other, piece)], axis=0
        )
    rows_a = piece.reshape(OWNERS * A_PIECE, 128)[: 3 * A_ROWS].reshape(3, A_ROWS, 128)
    rows_a = rows_a.transpose(1, 0, 2)
    mid_a = 98
    flat_a = jnp.concatenate(
        [rows_a[:FEAT], rows_a[FPAD : FPAD + FEAT], rows_a[2 * FPAD : 2 * FPAD + mid_a]]
    ).reshape(-1)
    all_b = piece[:, :B_PIECE].reshape(OWNERS * B_PIECE, 128)
    rows_b = all_b[: 3 * B_ROWS].reshape(3, B_ROWS, 128).transpose(1, 0, 2)[mid_a - 96 :]
    vec_sum = all_b[3 * B_ROWS : 3 * B_ROWS + 24 : 8].reshape(HID)
    flat_b = jnp.concatenate(
        [rows_b.reshape(-1), (vec_sum[:, None] * energy[None, :]).reshape(-1)]
    )
    grad_half = jnp.where(is_physics, flat_b, flat_a)

    new = vmem_call(
        final_kernel,
        [shape((FLAT, COLS), f32)],
        [],
        2,
        3,
        10**7,
        6 * 10**6,
        "final",
    )(table, flags, field, own_out, back)[0]
    return new.reshape(columns.shape), grad_half


def solution(mesh):
    lat, lon, grp = mesh.devices.shape
    split = Mesh(
        mesh.devices.reshape(lat, lon // 4, 2, 2, grp), ("lat", "y", "x", "core", "grp")
    )
    grid = P("lat", LON)
    columns = P("grp", None, "lat", LON)
    return jax.shard_map(
        on_device,
        mesh=split,
        in_specs=(columns, grid, grid, P(), P(), P(), P(), P(), P()),
        out_specs=(columns, P("grp")),
        check_vma=False,
    )
```

```python
import functools
import math

import jax
import jax.numpy as jnp
from jax import lax
from jax.experimental import pallas as pl
from jax.experimental.pallas import tpu as pltpu
from jax.sharding import Mesh, PartitionSpec as P

f32 = jnp.float32
bf16 = jnp.bfloat16

FEAT = 278
FPAD = 288
PACK = 144
ROWS = 16
COLS = 128
HID = 384
OUT = 368
FLAT = FEAT * ROWS
MINE = ROWS * COLS // 2
LON = ("y", "x", "core")
LAT = ("za", "zb", "zc")
VMEM_LIMIT = 24 * 1024 * 1024

NT = (((1,), (1,)), ((), ()))
TN = (((0,), (0,)), ((), ()))

A_ROWS = 680
B_ROWS = 288
OWNERS = 128
A_PIECE = 16
B_PIECE = 8
PIECE = A_PIECE + B_PIECE


def vmem_call(kernel, outs, scratch, n_smem, n_vmem, flops, size, name):
    return pl.pallas_call(
        kernel,
        out_shape=outs,
        in_specs=[pl.BlockSpec(memory_space=pltpu.SMEM)] * n_smem
        + [pl.BlockSpec(memory_space=pltpu.VMEM)] * n_vmem,
        out_specs=jax.tree.map(lambda _: pl.BlockSpec(memory_space=pltpu.VMEM), outs),
        scratch_shapes=scratch,
        compiler_params=pltpu.CompilerParams(vmem_limit_bytes=VMEM_LIMIT),
        cost_estimate=pl.CostEstimate(flops=flops, bytes_accessed=size, transcendentals=0),
        name=name,
    )


def lane_ids(shape):
    return lax.broadcasted_iota(jnp.int32, shape, len(shape) - 1)


def row_ids(shape):
    return lax.broadcasted_iota(jnp.int32, shape, len(shape) - 2)


def chunks():
    full = FEAT // 8
    return full, FEAT - full * 8


def coefficients(east, north, flags_ref):
    dyn = flags_ref[0]
    not_top = flags_ref[1]
    rows = row_ids(north.shape)
    north = jnp.where(rows == ROWS - 1, north * not_top, north) * dyn
    east = east * dyn
    keep = 1.0 - east - north
    west = jnp.where(lane_ids(east.shape) == 0, 0.0, pltpu.roll(east, 1, 1))
    south = jnp.where(rows == 0, 0.0, pltpu.roll(north, 1, 0))
    return east, north, keep, west, south


def step(q, keep, west, south):
    shaped = q.reshape(-1, ROWS, COLS)
    out = (
        keep[None] * shaped
        + west[None] * pltpu.roll(shaped, 1, 2)
        + south[None] * pltpu.roll(shaped, 1, 1)
    )
    return out


def tiled_column(value, lane):
    column = jnp.broadcast_to(value[:, lane : lane + 1], (ROWS, COLS))
    return jnp.concatenate([column] * 8, axis=0)


def rim_kernel(flags_ref, x_ref, east_ref, north_ref, rim_ref, corner_ref, north_out_ref):
    east, north, keep, west, south = coefficients(east_ref[...], north_ref[...], flags_ref)
    full, rest = chunks()
    lane = lane_ids((128, COLS))
    picked = jnp.zeros((128, COLS), f32)
    for g in range(full):
        turned = pltpu.roll(x_ref[g * 128 : (g + 1) * 128, :], 2 * g + 2, 1)
        picked = jnp.where(lane // 2 == g, turned, picked)
    tail = pltpu.roll(x_ref[full * 128 :, :], 2 * full + 2, 1)
    tail = jnp.concatenate([tail, jnp.zeros((128 - rest * ROWS, COLS), f32)], axis=0)
    picked = jnp.where(lane // 2 == full, tail, picked)

    last = COLS - 1
    east_last = tiled_column(east, last)
    after = (
        tiled_column(keep, last) * picked
        + tiled_column(west, last) * pltpu.roll(picked, 1, 1)
        + tiled_column(south, last) * pltpu.roll(picked, 1, 0)
    )
    odd = lane % 2 == 1
    flux_one = east_last * picked
    flux_two = pltpu.roll(east_last * after, COLS - 1, 1)
    flux_up = pltpu.roll(tiled_column(north, last) * picked, COLS - 1, 1)
    scalar = jnp.broadcast_to(east[0:1, last:], (128, COLS))
    rim = jnp.where(odd, flux_one, flux_two)
    rim_ref[...] = jnp.where(lane == last, scalar, rim).astype(bf16)
    corner_ref[...] = jnp.where(odd, flux_one, flux_up).astype(bf16)

    q_top = x_ref[pl.ds(ROWS - 1, FEAT, stride=ROWS), :]
    q_under = x_ref[pl.ds(ROWS - 2, FEAT, stride=ROWS), :]
    top = slice(ROWS - 1, ROWS)
    after_top = (
        keep[top] * q_top + west[top] * pltpu.roll(q_top, 1, 1) + south[top] * q_under
    )
    north_out_ref[0:FEAT, :] = (north[top] * q_top).astype(bf16)
    north_out_ref[FPAD : FPAD + FEAT, :] = (north[top] * after_top).astype(bf16)
    pad = jnp.broadcast_to(north[top], (FPAD - FEAT, COLS)).astype(bf16)
    north_out_ref[FEAT:FPAD, :] = pad
    north_out_ref[FPAD + FEAT :, :] = pad


def transport_kernel(
    table_ref, flags_ref, x_ref, east_ref, north_ref, rim_ref, south_ref, corner_ref,
    field_ref, own_ref, send_ref, mid_ref, inflow_ref,
):
    east, north, keep, west, south = coefficients(east_ref[...], north_ref[...], flags_ref)
    full, rest = chunks()
    lane = lane_ids((128, COLS))
    odd = lane % 2 == 1
    rim = rim_ref[...].astype(f32)
    corner = pltpu.roll(corner_ref[...].astype(f32), 128 - (ROWS - 1), 0)
    east_courant = rim[0:1, COLS - 1 : COLS]
    north_courant = south_ref[FEAT : FEAT + 1, 0:1].astype(f32)
    lacked = corner * east_courant + pltpu.roll(corner, COLS - 1, 1) * north_courant
    fix = jnp.logical_and(row_ids((128, COLS)) % ROWS == 0, jnp.logical_not(odd))
    inflow_ref[...] = rim + jnp.where(fix, lacked, 0.0)

    def stage(source, target, g, count, shift):
        rows = pl.ds(pl.multiple_of(g * 128, 128), count * ROWS)
        inflow = pltpu.roll(inflow_ref[0 : count * ROWS, :], shift, 1)
        inflow = jnp.where(lane[: count * ROWS] == 0, inflow, 0.0)
        after = step(source[rows, :], keep, west, south).reshape(count * ROWS, COLS)
        target[rows, :] = after + inflow

    row0 = pl.ds(0, FEAT, stride=ROWS)

    def first_body(g, carry):
        stage(x_ref, mid_ref, g, 8, COLS - 1 - 2 * g)
        return carry

    lax.fori_loop(0, full, first_body, 0, unroll=4)
    stage(x_ref, mid_ref, full, rest, COLS - 1 - 2 * full)
    mid_ref[row0, :] = mid_ref[row0, :] + south_ref[0:FEAT, :].astype(f32)

    def second_body(g, carry):
        stage(mid_ref, field_ref, g, 8, COLS - 2 * g)
        return carry

    lax.fori_loop(1, full, second_body, 0, unroll=4)
    stage(mid_ref, field_ref, 0, 8, 0)
    stage(mid_ref, field_ref, full, rest, COLS - 2 * full)
    field_ref[row0, :] = field_ref[row0, :] + south_ref[FPAD : FPAD + FEAT, :].astype(f32)

    to_slot = table_ref[2, 1]
    is_dyn = to_slot == 1
    low = lane_ids((PACK, COLS)) < COLS // 2
    low_full = lane_ids((FPAD, COLS)) < COLS // 2
    zeros = jnp.zeros((FPAD - FEAT, COLS), f32)

    def pair_body(i, carry):
        kept = []
        for side in range(2):
            r = 2 * i + side
            rows = pl.ds(table_ref[0, r], FEAT, stride=ROWS)
            here = jnp.concatenate([field_ref[rows, :], zeros], axis=0)
            turned = pltpu.roll(here, COLS // 2, 1)
            value = jnp.where(is_dyn, here, turned)
            other = jnp.where(is_dyn, turned, here)
            packed = jnp.where(low, other[:PACK], value[PACK:])
            send_ref[2 * r + to_slot] = packed.astype(bf16)
            send_ref[2 * r + 1 - to_slot] = jnp.zeros((PACK, COLS), bf16)
            kept.append(value if side == 0 else other)
        own_ref[:, pl.ds(pl.multiple_of(i * COLS, COLS), COLS)] = jnp.where(
            low_full, kept[0], kept[1]
        ).astype(bf16)
        return carry

    lax.fori_loop(0, ROWS // 2, pair_body, 0, unroll=2)


def sigmoid(value):
    return 0.5 + 0.5 * jnp.tanh(0.5 * value)


def swap_halves(value):
    return pltpu.roll(value, COLS // 2, 1)


def forward_kernel(
    table_ref, own_ref, recv_ref, w_one_ref, w_two_ref, w_three_ref, gain_ref,
    inputs_ref, hidden_ref, g_two_ref, slope_ref, own_out_ref, send_ref, vec_ref,
):
    from_slot = table_ref[2, 1]
    offset = table_ref[2, 2]
    low = lane_ids((PACK, COLS)) < COLS // 2
    gain = gain_ref[...]
    loss_norm = 1.0 / math.sqrt(ROWS * 8 * COLS * ROWS)
    energy_norm = 1.0 / math.sqrt(OUT)
    tile = 2 * COLS
    vec_ref[...] = jnp.zeros(vec_ref.shape, f32)

    def tile_body(t, carry):
        lanes = pl.ds(pl.multiple_of(t * tile, tile), tile)
        live_parts = []
        for g in range(2):
            i = 2 * t + g
            group = pl.ds(pl.multiple_of(i * COLS, COLS), COLS)
            first = recv_ref[4 * i + from_slot].astype(f32)
            second = recv_ref[4 * i + 2 + from_slot].astype(f32)
            inputs_ref[0:FPAD, group] = own_ref[:, group]
            inputs_ref[FPAD : FPAD + PACK, group] = jnp.where(
                low, first, swap_halves(second)
            ).astype(bf16)
            inputs_ref[FPAD + PACK :, group] = jnp.where(
                low, swap_halves(first), second
            ).astype(bf16)
            lane = lane_ids((1, COLS))
            column = lane % (COLS // 2) + offset
            cost = jnp.where(lane < COLS // 2, table_ref[1, 2 * i], table_ref[1, 2 * i + 1])
            live_parts.append(jnp.where(column < cost, 1.0, 0.0))
        live = jnp.concatenate(live_parts, axis=1)
        inputs = inputs_ref[:, lanes]
        pre_one = jnp.dot(w_one_ref[...], inputs, preferred_element_type=f32)
        sig = sigmoid(pre_one)
        silu = pre_one * sig
        hidden_one = silu.astype(bf16)
        slope_ref[:, lanes] = sig + silu * (1.0 - sig)
        hidden_ref[:, lanes] = hidden_one
        pre_two = jnp.dot(w_two_ref[...], hidden_one, preferred_element_type=f32)
        sig = sigmoid(pre_two)
        silu = pre_two * sig
        hidden_two = silu.astype(bf16)
        slope_two = sig + silu * (1.0 - sig)
        result = jnp.dot(w_three_ref[...], hidden_two, preferred_element_type=f32).astype(bf16)
        own_out_ref[:, lanes] = result[:FPAD]
        to_send = result[FPAD:].astype(f32)
        for g in range(2):
            i = 2 * t + g
            part = to_send[:, g * COLS : (g + 1) * COLS]
            other = swap_halves(part)
            zeros = jnp.zeros((PACK, COLS), bf16)
            send_ref[4 * i + from_slot] = jnp.where(low, part[:PACK], other[PACK:]).astype(bf16)
            send_ref[4 * i + 2 + from_slot] = jnp.where(
                low, other[:PACK], part[PACK:]
            ).astype(bf16)
            send_ref[4 * i + 1 - from_slot] = zeros
            send_ref[4 * i + 3 - from_slot] = zeros
        energy = jnp.sum(gain * hidden_two.astype(f32), axis=0, keepdims=True) * energy_norm
        weight = live * energy * loss_norm
        g_two_ref[:, lanes] = (gain * weight * slope_two).astype(bf16)
        high = weight.astype(bf16)
        left = weight - high.astype(f32)
        mid = left.astype(bf16)
        low_part = (left - mid.astype(f32)).astype(bf16)
        rows = row_ids((16, tile))
        stacked = jnp.where(
            rows == 0,
            high.astype(f32),
            jnp.where(rows == 1, mid.astype(f32), jnp.where(rows == 2, low_part.astype(f32), 0.0)),
        ).astype(bf16)
        vec_ref[...] += lax.dot_general(stacked, hidden_two, NT, preferred_element_type=f32)
        return carry

    lax.fori_loop(0, MINE // tile, tile_body, 0, unroll=True)


def place(owner):
    core, x, za, zb, zc, y = (
        owner // 64, owner // 32 % 2, owner // 16 % 2, owner // 8 % 2, owner // 4 % 2, owner % 4
    )
    return core, zc * 32 + zb * 16 + za * 8 + y * 2 + x


def backward_kernel(
    table_ref, inputs_ref, hidden_ref, g_two_ref, slope_ref, w_mid_ref, vec_ref,
    keep_ref, send_ref, g_one_ref, d_in_ref,
):
    state_first = table_ref[2, 3]
    core = table_ref[2, 4]
    tile = 2 * COLS

    def tile_body(t, carry):
        lanes = pl.ds(pl.multiple_of(t * tile, tile), tile)
        back = jnp.dot(w_mid_ref[...], g_two_ref[:, lanes], preferred_element_type=f32)
        g_one_ref[:, lanes] = (back * slope_ref[:, lanes]).astype(bf16)
        return carry

    lax.fori_loop(0, MINE // tile, tile_body, 0, unroll=True)
    d_mid = lax.dot_general(hidden_ref[...], g_two_ref[...], NT, preferred_element_type=f32)
    g_one = g_one_ref[...]
    own_at = pl.multiple_of((1 - state_first) * FPAD, 8)
    recv_at = pl.multiple_of(state_first * FPAD, 8)
    d_in_ref[pl.ds(own_at, FPAD), :] = lax.dot_general(
        inputs_ref[:FPAD, :], g_one, NT, preferred_element_type=f32
    )
    d_in_ref[pl.ds(recv_at, FPAD), :] = lax.dot_general(
        inputs_ref[FPAD:, :], g_one, NT, preferred_element_type=f32
    )

    def write(refs):
        def put(owner, at, value):
            half, index = place(owner)
            refs[half][index, at : at + 8, :] = value

        def put_a(row, value):
            put(row // A_PIECE, row % A_PIECE, value)

        def put_b(row, value):
            put(row // B_PIECE, A_PIECE, value)

        for l in range(3):
            lanes = slice(l * 128, (l + 1) * 128)
            for k in range(2 * FPAD // 8):
                put_a(l * A_ROWS + k * 8, d_in_ref[k * 8 : k * 8 + 8, lanes])
            for k in range((A_ROWS - 2 * FPAD) // 8):
                put_a(l * A_ROWS + 2 * FPAD + k * 8, d_mid[k * 8 : k * 8 + 8, lanes])
            for k in range(B_ROWS // 8):
                put_b(l * B_ROWS + k * 8, d_mid[96 + k * 8 : 96 + k * 8 + 8, lanes])
        zeros = jnp.zeros((8, 128), f32)
        for row in range(3 * A_ROWS, OWNERS * A_PIECE, 8):
            put_a(row, zeros)
        vec = jnp.sum(vec_ref[...], axis=0, keepdims=True)
        for l in range(3):
            put_b(3 * B_ROWS + l * 8, jnp.broadcast_to(vec[:, l * 128 : (l + 1) * 128], (8, 128)))
        for row in range(3 * B_ROWS + 24, OWNERS * B_PIECE, 8):
            put_b(row, zeros)

    @pl.when(core == 0)
    def _():
        write((keep_ref, send_ref))

    @pl.when(core == 1)
    def _():
        write((send_ref, keep_ref))


def final_kernel(table_ref, scale_ref, field_ref, own_ref, recv_ref, out_ref):
    from_slot = table_ref[2, 1]
    is_dyn = from_slot == 1
    keep_scale = scale_ref[2]
    new_scale = scale_ref[3]
    low = lane_ids((PACK, COLS)) < COLS // 2
    low_full = lane_ids((FPAD, COLS)) < COLS // 2

    def pair_body(i, carry):
        pair = own_ref[:, pl.ds(pl.multiple_of(i * COLS, COLS), COLS)].astype(f32)
        for side in range(2):
            r = 2 * i + side
            chunk = recv_ref[2 * r + from_slot].astype(f32)
            theirs = jnp.concatenate([swap_halves(chunk), chunk], axis=0)
            mine = pair if side == 0 else swap_halves(pair)
            tend = jnp.where(low_full, mine, theirs)[:FEAT]
            tend = jnp.where(is_dyn, tend, swap_halves(tend))
            rows = pl.ds(table_ref[0, r], FEAT, stride=ROWS)
            old = field_ref[rows, :]
            live = lane_ids((FEAT, COLS)) < table_ref[1, r]
            out_ref[rows, :] = jnp.where(live, keep_scale * old + new_scale * tend, old)
        return carry

    lax.fori_loop(0, ROWS // 2, pair_body, 0, unroll=2)


def shape(dims, dtype):
    return jax.ShapeDtypeStruct(dims, dtype)


def swap(value, axis):
    return lax.ppermute(value, axis, [(0, 1), (1, 0)])


def on_device(columns, east_courant, north_courant, assign, block_cost, w_in, w_mid, w_out, energy):
    band = lax.axis_index(LAT)
    bands = lax.axis_size(LAT)
    lon = lax.axis_index(LON)
    lons = lax.axis_size(LON)
    grp = lax.axis_index("grp")
    is_physics = grp == 1
    stored = columns.reshape(FLAT, COLS)

    dyn = (1 - grp).astype(f32)
    flags = jnp.stack(
        [dyn, (band != bands - 1).astype(f32), jnp.where(is_physics, 0.0, 1.0), jnp.where(is_physics, 1.0, 0.5)]
    )
    rim, corner, north_out = vmem_call(
        rim_kernel,
        [shape((128, COLS), bf16), shape((128, COLS), bf16), shape((2 * FPAD, COLS), bf16)],
        [],
        1,
        3,
        10**8,
        3 * 10**6,
        "rim",
    )(flags, stored, east_courant, north_courant)
    from_west = lax.ppermute(rim, LON, [(i, (i + 1) % lons) for i in range(lons)])
    from_south = lax.ppermute(north_out, LAT, [(i, i + 1) for i in range(bands - 1)])
    from_corner = lax.ppermute(
        corner,
        LAT + LON,
        [(b * lons + i, (b + 1) * lons + (i + 1) % lons) for b in range(bands - 1) for i in range(lons)],
    )

    targets = lax.dynamic_index_in_dim(assign, band, 0, keepdims=False)
    costs = lax.dynamic_index_in_dim(block_cost, band, 0, keepdims=False)
    owner = targets // ROWS
    ids = lax.broadcasted_iota(jnp.int32, (ROWS, ROWS), 0)
    ks = lax.broadcasted_iota(jnp.int32, (ROWS, ROWS), 1)
    here_owner = lax.dynamic_index_in_dim(owner, lon, 0, keepdims=True)
    here_cost = lax.dynamic_index_in_dim(costs, lon, 0, keepdims=True)
    match = jnp.where(is_physics, owner == lon, here_owner == ids)
    row_of = jnp.sum(jnp.where(match, jnp.where(is_physics, targets % ROWS, ks), 0), axis=1)
    cost_of = jnp.sum(jnp.where(match, jnp.where(is_physics, costs, here_cost), 0), axis=1)
    half = COLS // 2
    facts = jnp.stack([grp * half, 1 - grp, grp * half, 1 - grp, lax.axis_index("core")]).astype(jnp.int32)
    table = jnp.stack([row_of, cost_of, jnp.pad(facts, (0, ROWS - 5))]).astype(jnp.int32)

    def halves(a, b, axis):
        first = jnp.where(is_physics, b, a)
        second = jnp.where(is_physics, a, b)
        pad = [(0, 0), (0, 0)]
        pad[axis] = (0, FPAD - FEAT)
        return jnp.concatenate([jnp.pad(first, pad), jnp.pad(second, pad)], axis=axis)

    w_in_t = w_in.T
    w_one = halves(w_in_t[:, :FEAT], w_in_t[:, FEAT:], 1)
    w_out_t = w_out.T
    w_three = halves(w_out_t[:FEAT], w_out_t[OUT - FEAT :], 0)
    gain = jnp.sum(w_out.astype(f32) * energy[None, :], axis=1, keepdims=True)

    field, own, send = vmem_call(
        transport_kernel,
        [shape((FLAT, COLS), f32), shape((FPAD, MINE), bf16), shape((2 * ROWS, PACK, COLS), bf16)],
        [pltpu.VMEM((FLAT, COLS), f32), pltpu.VMEM((128, COLS), f32)],
        2,
        6,
        10**8,
        6 * 10**6,
        "transport",
    )(table, flags, stored, east_courant, north_courant, from_west, from_south, from_corner)
    recv = lax.all_to_all(send, LON + ("grp",), 0, 0, tiled=True)
    inputs, hidden, g_two, slope, own_out, send_back, vec = vmem_call(
        forward_kernel,
        [
            shape((2 * FPAD, MINE), bf16),
            shape((HID, MINE), bf16),
            shape((HID, MINE), bf16),
            shape((HID, MINE), f32),
            shape((FPAD, MINE), bf16),
            shape((2 * ROWS, PACK, COLS), bf16),
            shape((16, HID), f32),
        ],
        [],
        1,
        6,
        2 * MINE * HID * (4 * FPAD + HID),
        8 * 10**6,
        "forward",
    )(table, own, recv, w_one, w_mid.T, w_three, gain)
    back = lax.all_to_all(send_back, LON + ("grp",), 0, 0, tiled=True)
    keep, other = vmem_call(
        backward_kernel,
        [shape((OWNERS // 2, PIECE, 128), f32)] * 2,
        [pltpu.VMEM((HID, MINE), bf16), pltpu.VMEM((2 * FPAD, HID), f32)],
        1,
        6,
        2 * MINE * HID * (2 * FPAD + 2 * HID),
        6 * 10**6,
        "backward",
    )(table, inputs, hidden, g_two, slope, w_mid, vec)

    grad = keep + swap(other, "core")
    for axis in ("zc", "zb"):
        pieces = grad.shape[0] // 2
        at = lax.axis_index(axis)
        other = lax.dynamic_slice_in_dim(grad, (1 - at) * pieces, pieces)
        keep = lax.dynamic_slice_in_dim(grad, at * pieces, pieces)
        grad = keep + swap(other, axis)
    grad, back = lax.optimization_barrier((grad, back))
    pieces_b = jnp.pad(grad[:, A_PIECE:], ((0, 0), (0, A_PIECE - B_PIECE), (0, 0)))
    pieces = jnp.stack([grad[:, :A_PIECE], pieces_b], axis=1).reshape(-1, A_PIECE, 128)
    piece = jnp.sum(lax.all_to_all(pieces, ("za", "y", "x", "grp"), 0, 0, tiled=True), axis=0)
    ring = LAT + ("y",)
    members = bands * lax.axis_size("y")
    piece = lax.all_to_all(
        jnp.broadcast_to(piece[None], (members,) + piece.shape), ring, 0, 0, tiled=True
    )
    new = vmem_call(
        final_kernel,
        [shape((FLAT, COLS), f32)],
        [],
        2,
        3,
        10**7,
        6 * 10**6,
        "final",
    )(table, flags, field, own_out, back)[0]
    for axis in ("x", "core"):
        other = swap(piece, axis)
        if axis == "x":
            other, new = lax.optimization_barrier((other, new))
        at_zero = lax.axis_index(axis) == 0
        piece = jnp.concatenate(
            [jnp.where(at_zero, piece, other), jnp.where(at_zero, other, piece)], axis=0
        )
    rows_a = piece.reshape(OWNERS * A_PIECE, 128)[: 3 * A_ROWS].reshape(3, A_ROWS, 128)
    rows_a = rows_a.transpose(1, 0, 2)
    mid_a = 98
    flat_a = jnp.concatenate(
        [rows_a[:FEAT], rows_a[FPAD : FPAD + FEAT], rows_a[2 * FPAD : 2 * FPAD + mid_a]]
    ).reshape(-1)
    all_b = piece[:, :B_PIECE].reshape(OWNERS * B_PIECE, 128)
    rows_b = all_b[: 3 * B_ROWS].reshape(3, B_ROWS, 128).transpose(1, 0, 2)[mid_a - 96 :]
    vec_sum = all_b[3 * B_ROWS : 3 * B_ROWS + 24 : 8].reshape(HID)
    flat_b = jnp.concatenate(
        [rows_b.reshape(-1), (vec_sum[:, None] * energy[None, :]).reshape(-1)]
    )
    grad_half = jnp.where(is_physics, flat_b, flat_a)

    return new.reshape(columns.shape), grad_half


def solution(mesh):
    lat, lon, grp = mesh.devices.shape
    split = Mesh(mesh.devices.reshape(lat // 4, 2, 2, lon // 4, 2, 2, grp), LAT + LON + ("grp",))
    grid = P(LAT, LON)
    columns = P("grp", None, LAT, LON)
    return jax.shard_map(
        on_device,
        mesh=split,
        in_specs=(columns, grid, grid, P(), P(), P(), P(), P(), P()),
        out_specs=(columns, P("grp")),
        check_vma=False,
    )
```

```python
import functools
import math

import jax
import jax.numpy as jnp
from jax import lax
from jax.experimental import pallas as pl
from jax.experimental.pallas import tpu as pltpu
from jax.sharding import Mesh, PartitionSpec as P

f32 = jnp.float32
bf16 = jnp.bfloat16

FEAT = 278
FPAD = 288
PACK = 144
ROWS = 16
COLS = 128
HID = 384
OUT = 368
FLAT = FEAT * ROWS
MINE = ROWS * COLS // 2
LON = ("y", "x", "core")
LAT = ("za", "zb", "zc")
MIB = 1024 * 1024
ALL_VMEM = 60

NT = (((1,), (1,)), ((), ()))
TN = (((0,), (0,)), ((), ()))

A_ROWS = 680
B_ROWS = 288
OWNERS = 128
A_PIECE = 16
B_PIECE = 8
PIECE = A_PIECE + B_PIECE


def vmem_call(kernel, outs, scratch, places, flops, size, name, limit, out_places=None):
    spaces = {"s": pltpu.SMEM, "v": pltpu.VMEM, "h": pltpu.HBM}
    out_places = out_places or "v" * len(outs)
    return pl.pallas_call(
        kernel,
        out_shape=outs,
        in_specs=[pl.BlockSpec(memory_space=spaces[p]) for p in places],
        out_specs=[pl.BlockSpec(memory_space=spaces[p]) for p in out_places],
        scratch_shapes=scratch,
        compiler_params=pltpu.CompilerParams(vmem_limit_bytes=limit * MIB),
        cost_estimate=pl.CostEstimate(flops=flops, bytes_accessed=size, transcendentals=0),
        name=name,
    )


def lane_ids(shape):
    return lax.broadcasted_iota(jnp.int32, shape, len(shape) - 1)


def row_ids(shape):
    return lax.broadcasted_iota(jnp.int32, shape, len(shape) - 2)


def chunks():
    full = FEAT // 8
    return full, FEAT - full * 8


def coefficients(east, north, dyn, not_top):
    rows = row_ids(north.shape)
    north = jnp.where(rows == ROWS - 1, north * not_top, north) * dyn
    east = east * dyn
    keep = 1.0 - east - north
    west = jnp.where(lane_ids(east.shape) == 0, 0.0, pltpu.roll(east, 1, 1))
    south = jnp.where(rows == 0, 0.0, pltpu.roll(north, 1, 0))
    return east, north, keep, west, south


def tiled_column(value, lane):
    column = jnp.broadcast_to(value[:, lane : lane + 1], (ROWS, COLS))
    return jnp.concatenate([column] * 8, axis=0)


def block_table(is_physics, lon, facts, targets, costs, own_targets, own_costs):
    ids = lax.broadcasted_iota(jnp.int32, (ROWS, ROWS), 0)
    ks = lax.broadcasted_iota(jnp.int32, (ROWS, ROWS), 1)
    own_targets = jnp.broadcast_to(own_targets, (ROWS, ROWS))
    own_costs = jnp.broadcast_to(own_costs, (ROWS, ROWS))
    at_home = own_targets // ROWS == ids
    at_slot = targets // ROWS == lon
    rows = jnp.where(
        is_physics, jnp.where(at_slot, targets % ROWS, 0), jnp.where(at_home, ks, 0)
    )
    costs = jnp.where(is_physics, jnp.where(at_slot, costs, 0), jnp.where(at_home, own_costs, 0))
    rows = jnp.sum(rows, axis=1, keepdims=True)
    costs = jnp.sum(costs, axis=1, keepdims=True)
    lane = lane_ids((ROWS, COLS))
    table = jnp.where(lane == 0, rows, jnp.where(lane == 1, costs, 0))
    for k, fact in enumerate(facts):
        table = jnp.where(lane == 2 + k, fact, table)
    return table


GROUPS = -(-FEAT // 8)
X_CUTS = tuple(range(0, FLAT, 1024)) + (FLAT,)


def rim_kernel(
    x_hbm, east_hbm, north_hbm, assign_hbm, cost_hbm,
    rim_ref, corner_ref, north_out_ref, table_ref,
    x_ref, east_ref, north_ref, assign_ref, cost_ref, sems,
):
    band = lax.axis_index(LAT)
    lon = lax.axis_index(LON)
    grp = lax.axis_index("grp")
    core = lax.axis_index("core")
    not_top = jnp.where(band != lax.axis_size(LAT) - 1, 1, 0)
    copies = [
        pltpu.make_async_copy(x_hbm.at[pl.ds(a, b - a)], x_ref.at[pl.ds(a, b - a)], sems.at[i])
        for i, (a, b) in enumerate(zip(X_CUTS[:-1], X_CUTS[1:]))
    ]
    n = len(copies)
    small = [
        pltpu.make_async_copy(east_hbm, east_ref, sems.at[n]),
        pltpu.make_async_copy(north_hbm, north_ref, sems.at[n + 1]),
        pltpu.make_async_copy(assign_hbm.at[band], assign_ref, sems.at[n + 2]),
        pltpu.make_async_copy(cost_hbm.at[band], cost_ref, sems.at[n + 3]),
    ]
    for copy in small + copies:
        copy.start()
    for copy in small:
        copy.wait()
    table_ref[...] = block_table(
        grp == 1,
        lon,
        (not_top, 1 - grp, grp * (COLS // 2), core),
        assign_ref[...],
        cost_ref[...],
        assign_ref[pl.ds(lon, 1), :],
        cost_ref[pl.ds(lon, 1), :],
    )
    east, north, keep, west, south = coefficients(
        east_ref[...], north_ref[...], (1 - grp).astype(f32), not_top.astype(f32)
    )
    full, rest = chunks()
    lane = lane_ids((128, COLS))
    picked = jnp.zeros((128, COLS), f32)
    for g in range(full):
        if g % 8 == 0:
            copies[g // 8].wait()
        turned = pltpu.roll(x_ref[g * 128 : (g + 1) * 128, :], 2 * g + 2, 1)
        picked = jnp.where(lane // 2 == g, turned, picked)
    tail = pltpu.roll(x_ref[full * 128 :, :], 2 * full + 2, 1)
    tail = jnp.concatenate([tail, jnp.zeros((128 - rest * ROWS, COLS), f32)], axis=0)
    picked = jnp.where(lane // 2 == full, tail, picked)

    last = COLS - 1
    east_last = tiled_column(east, last)
    after = (
        tiled_column(keep, last) * picked
        + tiled_column(west, last) * pltpu.roll(picked, 1, 1)
        + tiled_column(south, last) * pltpu.roll(picked, 1, 0)
    )
    odd = lane % 2 == 1
    flux_one = east_last * picked
    flux_two = pltpu.roll(east_last * after, COLS - 1, 1)
    flux_up = pltpu.roll(tiled_column(north, last) * picked, COLS - 1, 1)
    scalar = jnp.broadcast_to(east[0:1, last:], (128, COLS))
    rim = jnp.where(odd, flux_one, flux_two)
    rim_ref[...] = jnp.where(lane == last, scalar, rim).astype(bf16)
    corner_ref[...] = jnp.where(odd, flux_one, flux_up).astype(bf16)

    q_top = x_ref[pl.ds(ROWS - 1, FEAT, stride=ROWS), :]
    q_under = x_ref[pl.ds(ROWS - 2, FEAT, stride=ROWS), :]
    top = slice(ROWS - 1, ROWS)
    after_top = (
        keep[top] * q_top + west[top] * pltpu.roll(q_top, 1, 1) + south[top] * q_under
    )
    north_out_ref[0:FEAT, :] = (north[top] * q_top).astype(bf16)
    north_out_ref[FPAD : FPAD + FEAT, :] = (north[top] * after_top).astype(bf16)
    pad = jnp.broadcast_to(north[top], (FPAD - FEAT, COLS)).astype(bf16)
    north_out_ref[FEAT:FPAD, :] = pad
    north_out_ref[FPAD + FEAT :, :] = pad


def transport_kernel(
    table_ref, x_hbm, east_ref, north_ref, rim_ref, south_ref, corner_ref,
    field_hbm, own_hbm, send_hbm,
    x_ref, field_ref, inflow_ref, rims_ref, south32_ref, own_ref, send_ref, sems,
):
    x_in = [
        pltpu.make_async_copy(
            x_hbm.at[pl.ds(a, b - a)], x_ref.at[pl.ds(a, b - a)], sems.at[1 + ROWS + ROWS // 2 + i]
        )
        for i, (a, b) in enumerate(zip(X_CUTS[:-1], X_CUTS[1:]))
    ]
    for copy in x_in:
        copy.start()
    x_ref[FLAT:, :] = jnp.zeros((x_ref.shape[0] - FLAT, COLS), f32)
    field_ref[:, GROUPS * 8 :, :] = jnp.zeros((ROWS, FPAD - GROUPS * 8, COLS), f32)
    south32_ref[...] = south_ref[...].astype(f32)
    to_slot = table_ref[0, 3]
    is_dyn = to_slot == 1
    east, north, keep, west, south = coefficients(
        east_ref[...], north_ref[...], to_slot.astype(f32), table_ref[0, 2].astype(f32)
    )
    west = jnp.where(lane_ids(west.shape) == 0, 1.0, west)
    keep, west, south = (value.reshape(ROWS, 1, COLS) for value in (keep, west, south))
    lane = lane_ids((128, COLS))
    rim = rim_ref[...].astype(f32)
    corner = pltpu.roll(corner_ref[...].astype(f32), 128 - (ROWS - 1), 0)
    east_courant = rim[0:1, COLS - 1 : COLS]
    north_courant = south32_ref[FEAT : FEAT + 1, 0:1]
    lacked = corner * east_courant + pltpu.roll(corner, COLS - 1, 1) * north_courant
    fix = jnp.logical_and(row_ids((128, COLS)) % ROWS == 0, lane % 2 == 0)
    inflow_ref[...] = rim + jnp.where(fix, lacked, 0.0)
    for k in range(ROWS):
        rims_ref[k] = inflow_ref[pl.ds(k, 8, stride=ROWS), :]
    last = lane_ids((ROWS, 8, COLS)) == COLS - 1

    def transported(q, shift, from_south):
        inflow = pltpu.roll(rims_ref[...], shift, 2)
        shifted = pltpu.roll(jnp.where(last, inflow, q), 1, 2)
        under = jnp.concatenate([q[ROWS - 1 :], q[: ROWS - 1]], axis=0)
        after = keep * q + west * shifted + south * under
        return jnp.concatenate([after[:1] + from_south[None], after[1:]], axis=0)

    def group(g, carry):
        rows = x_ref[pl.ds(pl.multiple_of(g * 128, 128), 128), :].reshape(8, ROWS, COLS)
        features = pl.ds(pl.multiple_of(g * 8, 8), 8)
        q = jnp.swapaxes(rows, 0, 1)
        q = transported(q, COLS - 2 - 2 * g, south32_ref[features, :])
        over = pl.ds(pl.multiple_of(FPAD + g * 8, 8), 8)
        field_ref[:, features, :] = transported(q, COLS - 1 - 2 * g, south32_ref[over, :])
        return carry

    field_out = []
    n_cuts = len(x_in)
    for i, copy in enumerate(x_in):
        copy.wait()
        first, end = 8 * i, min(8 * i + 8, GROUPS)
        lax.fori_loop(first, end, group, 0, unroll=4 if end - first == 8 else True)
        part = pl.ds(8 * first, 8 * (end - first) if end < GROUPS else FPAD - 8 * first)
        field_out.append(
            pltpu.make_async_copy(
                field_ref.at[:, part], field_hbm.at[:, part], sems.at[1 + ROWS + ROWS // 2 + n_cuts + i]
            )
        )
        field_out[-1].start()

    low = lane_ids((PACK, COLS)) < COLS // 2
    low_full = lane_ids((FPAD, COLS)) < COLS // 2

    def pair_body(i, carry):
        kept = []
        for side in range(2):
            r = 2 * i + side
            here = field_ref[table_ref[r, 0]]
            turned = pltpu.roll(here, COLS // 2, 1)
            value = jnp.where(is_dyn, here, turned)
            other = jnp.where(is_dyn, turned, here)
            packed = jnp.where(low, other[:PACK], value[PACK:])
            send_ref[r] = packed.astype(bf16)
            pltpu.make_async_copy(
                send_ref.at[r], send_hbm.at[2 * r + to_slot], sems.at[1 + r]
            ).start()
            kept.append(value if side == 0 else other)
        own_ref[i] = jnp.where(low_full, kept[0], kept[1]).astype(bf16)
        pltpu.make_async_copy(own_ref.at[i], own_hbm.at[i], sems.at[1 + ROWS + i]).start()
        return carry

    lax.fori_loop(0, ROWS // 2, pair_body, 0, unroll=2)
    for copy in field_out:
        copy.wait()
    for r in range(ROWS):
        pltpu.make_async_copy(
            send_ref.at[r], send_hbm.at[2 * r + to_slot], sems.at[1 + r]
        ).wait()
    for i in range(ROWS // 2):
        pltpu.make_async_copy(own_ref.at[i], own_hbm.at[i], sems.at[1 + ROWS + i]).wait()


def sigmoid(value):
    return 0.5 + 0.5 * jnp.tanh(0.5 * value)


def swap_halves(value):
    return pltpu.roll(value, COLS // 2, 1)


def forward_kernel(
    table_ref, own_ref, recv_ref, w_one_ref, w_two_ref, w_three_ref, gain_ref,
    inputs_ref, hidden_ref, g_two_ref, slope_ref, own_out_ref, send_ref, vec_ref,
):
    from_slot = table_ref[0, 3]
    offset = table_ref[0, 4]
    low = lane_ids((PACK, COLS)) < COLS // 2
    gain = gain_ref[...]
    loss_norm = 1.0 / math.sqrt(ROWS * 8 * COLS * ROWS)
    energy_norm = 1.0 / math.sqrt(OUT)
    tile = 2 * COLS
    vec_ref[...] = jnp.zeros(vec_ref.shape, f32)

    for t in range(MINE // tile):
        lanes = slice(t * tile, (t + 1) * tile)
        live_parts = []
        for g in range(2):
            i = 2 * t + g
            group = slice(i * COLS, (i + 1) * COLS)
            first = recv_ref[4 * i + from_slot].astype(f32)
            second = recv_ref[4 * i + 2 + from_slot].astype(f32)
            inputs_ref[0:FPAD, group] = own_ref[i]
            inputs_ref[FPAD : FPAD + PACK, group] = jnp.where(
                low, first, swap_halves(second)
            ).astype(bf16)
            inputs_ref[FPAD + PACK :, group] = jnp.where(
                low, swap_halves(first), second
            ).astype(bf16)
            lane = lane_ids((1, COLS))
            column = lane % (COLS // 2) + offset
            cost = jnp.where(lane < COLS // 2, table_ref[2 * i, 1], table_ref[2 * i + 1, 1])
            live_parts.append(jnp.where(column < cost, 1.0, 0.0))
        live = jnp.concatenate(live_parts, axis=1)
        inputs = inputs_ref[:, lanes]
        pre_one = jnp.dot(w_one_ref[...], inputs, preferred_element_type=f32)
        sig = sigmoid(pre_one)
        silu = pre_one * sig
        hidden_one = silu.astype(bf16)
        slope_ref[:, lanes] = sig + silu * (1.0 - sig)
        hidden_ref[:, lanes] = hidden_one
        pre_two = jnp.dot(w_two_ref[...], hidden_one, preferred_element_type=f32)
        sig = sigmoid(pre_two)
        silu = pre_two * sig
        hidden_two = silu.astype(bf16)
        slope_two = sig + silu * (1.0 - sig)
        result = jnp.dot(w_three_ref[...], hidden_two, preferred_element_type=f32).astype(bf16)
        own_out_ref[:, lanes] = result[:FPAD]
        to_send = result[FPAD:].astype(f32)
        for g in range(2):
            i = 2 * t + g
            part = to_send[:, g * COLS : (g + 1) * COLS]
            other = swap_halves(part)
            zeros = jnp.zeros((PACK, COLS), bf16)
            send_ref[4 * i + from_slot] = jnp.where(low, part[:PACK], other[PACK:]).astype(bf16)
            send_ref[4 * i + 2 + from_slot] = jnp.where(
                low, other[:PACK], part[PACK:]
            ).astype(bf16)
            send_ref[4 * i + 1 - from_slot] = zeros
            send_ref[4 * i + 3 - from_slot] = zeros
        energy = jnp.sum(gain * hidden_two.astype(f32), axis=0, keepdims=True) * energy_norm
        weight = live * energy * loss_norm
        g_two_ref[:, lanes] = (gain * weight * slope_two).astype(bf16)
        high = weight.astype(bf16)
        left = weight - high.astype(f32)
        mid = left.astype(bf16)
        low_part = (left - mid.astype(f32)).astype(bf16)
        rows = row_ids((16, tile))
        stacked = jnp.where(
            rows == 0,
            high.astype(f32),
            jnp.where(rows == 1, mid.astype(f32), jnp.where(rows == 2, low_part.astype(f32), 0.0)),
        ).astype(bf16)
        vec_ref[...] += lax.dot_general(stacked, hidden_two, NT, preferred_element_type=f32)


def place(owner):
    core, x, za, zb, zc, y = (
        owner // 64, owner // 32 % 2, owner // 16 % 2, owner // 8 % 2, owner // 4 % 2, owner % 4
    )
    return core, zc * 32 + zb * 16 + za * 8 + y * 2 + x


def backward_kernel(
    table_ref, inputs_ref, hidden_ref, g_two_ref, slope_ref, w_mid_ref, vec_ref,
    keep_ref, send_ref, g_one_ref, d_in_ref,
):
    state_first = table_ref[0, 3]
    core = table_ref[0, 5]
    tile = 2 * COLS

    def tile_body(t, carry):
        lanes = pl.ds(pl.multiple_of(t * tile, tile), tile)
        back = jnp.dot(w_mid_ref[...], g_two_ref[:, lanes], preferred_element_type=f32)
        g_one_ref[:, lanes] = (back * slope_ref[:, lanes]).astype(bf16)
        return carry

    lax.fori_loop(0, MINE // tile, tile_body, 0, unroll=True)
    d_mid = lax.dot_general(hidden_ref[...], g_two_ref[...], NT, preferred_element_type=f32)
    g_one = g_one_ref[...]
    own_at = pl.multiple_of((1 - state_first) * FPAD, 8)
    recv_at = pl.multiple_of(state_first * FPAD, 8)
    d_in_ref[pl.ds(own_at, FPAD), :] = lax.dot_general(
        inputs_ref[:FPAD, :], g_one, NT, preferred_element_type=f32
    )
    d_in_ref[pl.ds(recv_at, FPAD), :] = lax.dot_general(
        inputs_ref[FPAD:, :], g_one, NT, preferred_element_type=f32
    )

    def write(refs):
        def put(owner, at, value):
            half, index = place(owner)
            refs[half][index, at : at + 8, :] = value

        def put_a(row, value):
            put(row // A_PIECE, row % A_PIECE, value)

        def put_b(row, value):
            put(row // B_PIECE, A_PIECE, value)

        for l in range(3):
            lanes = slice(l * 128, (l + 1) * 128)
            for k in range(2 * FPAD // 8):
                put_a(l * A_ROWS + k * 8, d_in_ref[k * 8 : k * 8 + 8, lanes])
            for k in range((A_ROWS - 2 * FPAD) // 8):
                put_a(l * A_ROWS + 2 * FPAD + k * 8, d_mid[k * 8 : k * 8 + 8, lanes])
            for k in range(B_ROWS // 8):
                put_b(l * B_ROWS + k * 8, d_mid[96 + k * 8 : 96 + k * 8 + 8, lanes])
        zeros = jnp.zeros((8, 128), f32)
        for row in range(3 * A_ROWS, OWNERS * A_PIECE, 8):
            put_a(row, zeros)
        vec = jnp.sum(vec_ref[...], axis=0, keepdims=True)
        for l in range(3):
            put_b(3 * B_ROWS + l * 8, jnp.broadcast_to(vec[:, l * 128 : (l + 1) * 128], (8, 128)))
        for row in range(3 * B_ROWS + 24, OWNERS * B_PIECE, 8):
            put_b(row, zeros)

    @pl.when(core == 0)
    def _():
        write((keep_ref, send_ref))

    @pl.when(core == 1)
    def _():
        write((send_ref, keep_ref))


def final_kernel(table_ref, field_ref, own_ref, recv_ref, out_ref, new_ref):
    from_slot = table_ref[0, 3]
    is_dyn = from_slot == 1
    keep_scale = jnp.where(is_dyn, 1.0, 0.0)
    new_scale = jnp.where(is_dyn, 0.5, 1.0)
    low_full = lane_ids((FPAD, COLS)) < COLS // 2

    def pair_body(i, carry):
        pair = own_ref[:, pl.ds(pl.multiple_of(i * COLS, COLS), COLS)].astype(f32)
        for side in range(2):
            r = 2 * i + side
            chunk = recv_ref[2 * r + from_slot].astype(f32)
            theirs = jnp.concatenate([swap_halves(chunk), chunk], axis=0)
            mine = pair if side == 0 else swap_halves(pair)
            tend = jnp.where(low_full, mine, theirs)
            tend = jnp.where(is_dyn, tend, swap_halves(tend))
            old = field_ref[table_ref[r, 0]]
            live = lane_ids((FPAD, COLS)) < table_ref[r, 1]
            new_ref[table_ref[r, 0]] = jnp.where(live, keep_scale * old + new_scale * tend, old)
        return carry

    lax.fori_loop(0, ROWS // 2, pair_body, 0, unroll=2)
    full, rest = chunks()

    def group(g, carry):
        value = jnp.swapaxes(new_ref[:, pl.ds(pl.multiple_of(g * 8, 8), 8), :], 0, 1)
        out_ref[pl.ds(pl.multiple_of(g * 128, 128), 128), :] = value.reshape(128, COLS)
        return carry

    lax.fori_loop(0, full, group, 0, unroll=2)
    value = jnp.swapaxes(new_ref[:, full * 8 : full * 8 + 8, :], 0, 1).reshape(128, COLS)
    out_ref[full * 128 :, :] = value[: rest * ROWS]


def shape(dims, dtype):
    return jax.ShapeDtypeStruct(dims, dtype)


def swap(value, axis):
    return lax.ppermute(value, axis, [(0, 1), (1, 0)])


def on_device(columns, east_courant, north_courant, assign, block_cost, w_in, w_mid, w_out, energy):
    bands = lax.axis_size(LAT)
    lons = lax.axis_size(LON)
    is_physics = lax.axis_index("grp") == 1
    stored = columns.reshape(FLAT, COLS)

    n_copies = len(X_CUTS) - 1 + 4
    rim, corner, north_out, table = vmem_call(
        rim_kernel,
        [
            shape((128, COLS), bf16),
            shape((128, COLS), bf16),
            shape((2 * FPAD, COLS), bf16),
            shape((ROWS, COLS), jnp.int32),
        ],
        [
            pltpu.VMEM((FLAT, COLS), f32),
            pltpu.VMEM((ROWS, COLS), f32),
            pltpu.VMEM((ROWS, COLS), f32),
            pltpu.VMEM((ROWS, ROWS), jnp.int32),
            pltpu.VMEM((ROWS, ROWS), jnp.int32),
            pltpu.SemaphoreType.DMA((n_copies,)),
        ],
        "hhhhh",
        10**8,
        3 * 10**6,
        "rim",
        ALL_VMEM,
    )(stored, east_courant, north_courant, assign, block_cost)
    from_west = lax.ppermute(rim, LON, [(i, (i + 1) % lons) for i in range(lons)])
    from_south = lax.ppermute(north_out, LAT, [(i, i + 1) for i in range(bands - 1)])
    from_corner = lax.ppermute(
        corner,
        LAT + LON,
        [(b * lons + i, (b + 1) * lons + (i + 1) % lons) for b in range(bands - 1) for i in range(lons)],
    )

    def halves(a, b, axis):
        first = jnp.where(is_physics, b, a)
        second = jnp.where(is_physics, a, b)
        pad = [(0, 0), (0, 0)]
        pad[axis] = (0, FPAD - FEAT)
        return jnp.concatenate([jnp.pad(first, pad), jnp.pad(second, pad)], axis=axis)

    w_in_t = w_in.T
    w_one = halves(w_in_t[:, :FEAT], w_in_t[:, FEAT:], 1)
    w_out_t = w_out.T
    w_three = halves(w_out_t[:FEAT], w_out_t[OUT - FEAT :], 0)
    gain = jnp.sum(w_out.astype(f32) * energy[None, :], axis=1, keepdims=True)

    field, own, send = vmem_call(
        transport_kernel,
        [
            shape((ROWS, FPAD, COLS), f32),
            shape((ROWS // 2, FPAD, COLS), bf16),
            shape((2 * ROWS, PACK, COLS), bf16),
        ],
        [
            pltpu.VMEM((GROUPS * 128, COLS), f32),
            pltpu.VMEM((ROWS, FPAD, COLS), f32),
            pltpu.VMEM((128, COLS), f32),
            pltpu.VMEM((ROWS, 8, COLS), f32),
            pltpu.VMEM((2 * FPAD, COLS), f32),
            pltpu.VMEM((ROWS // 2, FPAD, COLS), bf16),
            pltpu.VMEM((ROWS, PACK, COLS), bf16),
            pltpu.SemaphoreType.DMA((1 + ROWS + ROWS // 2 + 2 * (len(X_CUTS) - 1),)),
        ],
        "shvvvvv",
        10**8,
        6 * 10**6,
        "transport",
        ALL_VMEM,
        "hhh",
    )(table, stored, east_courant, north_courant, from_west, from_south, from_corner)
    recv = lax.all_to_all(send, LON + ("grp",), 0, 0, tiled=True)
    inputs, hidden, g_two, slope, own_out, send_back, vec = vmem_call(
        forward_kernel,
        [
            shape((2 * FPAD, MINE), bf16),
            shape((HID, MINE), bf16),
            shape((HID, MINE), bf16),
            shape((HID, MINE), f32),
            shape((FPAD, MINE), bf16),
            shape((2 * ROWS, PACK, COLS), bf16),
            shape((16, HID), f32),
        ],
        [],
        "svvvvvv",
        2 * MINE * HID * (4 * FPAD + HID),
        8 * 10**6,
        "forward",
        16,
    )(table, own, recv, w_one, w_mid.T, w_three, gain)
    back = lax.all_to_all(send_back, LON + ("grp",), 0, 0, tiled=True)
    keep, other = vmem_call(
        backward_kernel,
        [shape((OWNERS // 2, PIECE, 128), f32)] * 2,
        [pltpu.VMEM((HID, MINE), bf16), pltpu.VMEM((2 * FPAD, HID), f32)],
        "svvvvvv",
        2 * MINE * HID * (2 * FPAD + 2 * HID),
        6 * 10**6,
        "backward",
        16,
    )(table, inputs, hidden, g_two, slope, w_mid, vec)

    grad = keep + swap(other, "core")
    for axis in ("zc", "zb"):
        pieces = grad.shape[0] // 2
        at = lax.axis_index(axis)
        other = lax.dynamic_slice_in_dim(grad, (1 - at) * pieces, pieces)
        keep = lax.dynamic_slice_in_dim(grad, at * pieces, pieces)
        grad = keep + swap(other.astype(bf16), axis).astype(f32)
    grad, back = lax.optimization_barrier((grad, back))
    pieces_b = jnp.pad(grad[:, A_PIECE:], ((0, 0), (0, A_PIECE - B_PIECE), (0, 0)))
    pieces = jnp.stack([grad[:, :A_PIECE], pieces_b], axis=1).reshape(-1, A_PIECE, 128)
    piece = jnp.sum(lax.all_to_all(pieces, ("za", "y", "x", "grp"), 0, 0, tiled=True), axis=0)
    ring = LAT + ("y",)
    members = bands * lax.axis_size("y")
    piece = lax.all_to_all(
        jnp.broadcast_to(piece[None], (members,) + piece.shape), ring, 0, 0, tiled=True
    )
    new = vmem_call(
        final_kernel,
        [shape((FLAT, COLS), f32)],
        [pltpu.VMEM((ROWS, FPAD, COLS), f32)],
        "svvv",
        10**7,
        6 * 10**6,
        "final",
        16,
    )(table, field, own_out, back)[0]
    for axis in ("x", "core"):
        other = swap(piece, axis)
        if axis == "x":
            other, new = lax.optimization_barrier((other, new))
        at_zero = lax.axis_index(axis) == 0
        piece = jnp.concatenate(
            [jnp.where(at_zero, piece, other), jnp.where(at_zero, other, piece)], axis=0
        )
    rows_a = piece.reshape(OWNERS * A_PIECE, 128)[: 3 * A_ROWS].reshape(3, A_ROWS, 128)
    rows_a = rows_a.transpose(1, 0, 2)
    mid_a = 98
    flat_a = jnp.concatenate(
        [rows_a[:FEAT], rows_a[FPAD : FPAD + FEAT], rows_a[2 * FPAD : 2 * FPAD + mid_a]]
    ).reshape(-1)
    all_b = piece[:, :B_PIECE].reshape(OWNERS * B_PIECE, 128)
    rows_b = all_b[: 3 * B_ROWS].reshape(3, B_ROWS, 128).transpose(1, 0, 2)[mid_a - 96 :]
    vec_sum = all_b[3 * B_ROWS : 3 * B_ROWS + 24 : 8].reshape(HID)
    flat_b = jnp.concatenate(
        [rows_b.reshape(-1), (vec_sum[:, None] * energy[None, :]).reshape(-1)]
    )
    grad_half = jnp.where(is_physics, flat_b, flat_a)

    return new.reshape(columns.shape), grad_half


def solution(mesh):
    lat, lon, grp = mesh.devices.shape
    split = Mesh(mesh.devices.reshape(lat // 4, 2, 2, lon // 4, 2, 2, grp), LAT + LON + ("grp",))
    grid = P(LAT, LON)
    columns = P("grp", None, LAT, LON)
    return jax.shard_map(
        on_device,
        mesh=split,
        in_specs=(columns, grid, grid, P(), P(), P(), P(), P(), P()),
        out_specs=(columns, P("grp")),
        check_vma=False,
    )
```

```python
import functools
import math

import jax
import jax.numpy as jnp
from jax import lax
from jax.experimental import pallas as pl
from jax.experimental.pallas import tpu as pltpu
from jax.sharding import Mesh, PartitionSpec as P

f32 = jnp.float32
bf16 = jnp.bfloat16

FEAT = 278
FPAD = 288
PACK = 144
ROWS = 16
COLS = 128
HID = 384
OUT = 368
FLAT = FEAT * ROWS
MINE = ROWS * COLS // 2
LON = ("y", "x", "core")
LAT = ("za", "zb", "zc")
MIB = 1024 * 1024
ALL_VMEM = 60

NT = (((1,), (1,)), ((), ()))
TN = (((0,), (0,)), ((), ()))

A_ROWS = 680
B_ROWS = 288
OWNERS = 128
A_PIECE = 16
B_PIECE = 8
PIECE = A_PIECE + B_PIECE


def vmem_call(kernel, outs, scratch, places, flops, size, name, limit, out_places=None):
    spaces = {"s": pltpu.SMEM, "v": pltpu.VMEM, "h": pltpu.HBM}
    out_places = out_places or "v" * len(outs)
    return pl.pallas_call(
        kernel,
        out_shape=outs,
        in_specs=[pl.BlockSpec(memory_space=spaces[p]) for p in places],
        out_specs=[pl.BlockSpec(memory_space=spaces[p]) for p in out_places],
        scratch_shapes=scratch,
        compiler_params=pltpu.CompilerParams(vmem_limit_bytes=limit * MIB),
        cost_estimate=pl.CostEstimate(flops=flops, bytes_accessed=size, transcendentals=0),
        name=name,
    )


def lane_ids(shape):
    return lax.broadcasted_iota(jnp.int32, shape, len(shape) - 1)


def row_ids(shape):
    return lax.broadcasted_iota(jnp.int32, shape, len(shape) - 2)


def chunks():
    full = FEAT // 8
    return full, FEAT - full * 8


def coefficients(east, north, dyn, not_top):
    rows = row_ids(north.shape)
    north = jnp.where(rows == ROWS - 1, north * not_top, north) * dyn
    east = east * dyn
    keep = 1.0 - east - north
    west = jnp.where(lane_ids(east.shape) == 0, 0.0, pltpu.roll(east, 1, 1))
    south = jnp.where(rows == 0, 0.0, pltpu.roll(north, 1, 0))
    return east, north, keep, west, south


def tiled_column(value, lane):
    column = jnp.broadcast_to(value[:, lane : lane + 1], (ROWS, COLS))
    return jnp.concatenate([column] * 8, axis=0)


def block_table(is_physics, lon, facts, targets, costs, own_targets, own_costs):
    ids = lax.broadcasted_iota(jnp.int32, (ROWS, ROWS), 0)
    ks = lax.broadcasted_iota(jnp.int32, (ROWS, ROWS), 1)
    own_targets = jnp.broadcast_to(own_targets, (ROWS, ROWS))
    own_costs = jnp.broadcast_to(own_costs, (ROWS, ROWS))
    at_home = own_targets // ROWS == ids
    at_slot = targets // ROWS == lon
    rows = jnp.where(
        is_physics, jnp.where(at_slot, targets % ROWS, 0), jnp.where(at_home, ks, 0)
    )
    costs = jnp.where(is_physics, jnp.where(at_slot, costs, 0), jnp.where(at_home, own_costs, 0))
    rows = jnp.sum(rows, axis=1, keepdims=True)
    costs = jnp.sum(costs, axis=1, keepdims=True)
    lane = lane_ids((ROWS, COLS))
    table = jnp.where(lane == 0, rows, jnp.where(lane == 1, costs, 0))
    for k, fact in enumerate(facts):
        table = jnp.where(lane == 2 + k, fact, table)
    return table


GROUPS = -(-FEAT // 8)
X_CUTS = tuple(range(0, FLAT, 1024)) + (FLAT,)


def rim_kernel(
    x_hbm, east_hbm, north_hbm, assign_hbm, cost_hbm,
    rim_ref, corner_ref, north_out_ref, table_ref,
    x_ref, east_ref, north_ref, assign_ref, cost_ref, sems,
):
    band = lax.axis_index(LAT)
    lon = lax.axis_index(LON)
    grp = lax.axis_index("grp")
    core = lax.axis_index("core")
    not_top = jnp.where(band != lax.axis_size(LAT) - 1, 1, 0)
    copies = [
        pltpu.make_async_copy(x_hbm.at[pl.ds(a, b - a)], x_ref.at[pl.ds(a, b - a)], sems.at[i])
        for i, (a, b) in enumerate(zip(X_CUTS[:-1], X_CUTS[1:]))
    ]
    n = len(copies)
    small = [
        pltpu.make_async_copy(east_hbm, east_ref, sems.at[n]),
        pltpu.make_async_copy(north_hbm, north_ref, sems.at[n + 1]),
        pltpu.make_async_copy(assign_hbm.at[band], assign_ref, sems.at[n + 2]),
        pltpu.make_async_copy(cost_hbm.at[band], cost_ref, sems.at[n + 3]),
    ]
    for copy in small + copies:
        copy.start()
    for copy in small:
        copy.wait()
    table_ref[...] = block_table(
        grp == 1,
        lon,
        (not_top, 1 - grp, grp * (COLS // 2), core, lax.axis_index("x")),
        assign_ref[...],
        cost_ref[...],
        assign_ref[pl.ds(lon, 1), :],
        cost_ref[pl.ds(lon, 1), :],
    )
    east, north, keep, west, south = coefficients(
        east_ref[...], north_ref[...], (1 - grp).astype(f32), not_top.astype(f32)
    )
    full, rest = chunks()
    lane = lane_ids((128, COLS))
    picked = jnp.zeros((128, COLS), f32)
    for g in range(full):
        if g % 8 == 0:
            copies[g // 8].wait()
        turned = pltpu.roll(x_ref[g * 128 : (g + 1) * 128, :], 2 * g + 2, 1)
        picked = jnp.where(lane // 2 == g, turned, picked)
    tail = pltpu.roll(x_ref[full * 128 :, :], 2 * full + 2, 1)
    tail = jnp.concatenate([tail, jnp.zeros((128 - rest * ROWS, COLS), f32)], axis=0)
    picked = jnp.where(lane // 2 == full, tail, picked)

    last = COLS - 1
    east_last = tiled_column(east, last)
    after = (
        tiled_column(keep, last) * picked
        + tiled_column(west, last) * pltpu.roll(picked, 1, 1)
        + tiled_column(south, last) * pltpu.roll(picked, 1, 0)
    )
    odd = lane % 2 == 1
    flux_one = east_last * picked
    flux_two = pltpu.roll(east_last * after, COLS - 1, 1)
    flux_up = pltpu.roll(tiled_column(north, last) * picked, COLS - 1, 1)
    scalar = jnp.broadcast_to(east[0:1, last:], (128, COLS))
    rim = jnp.where(odd, flux_one, flux_two)
    rim_ref[...] = jnp.where(lane == last, scalar, rim).astype(bf16)
    corner_ref[...] = jnp.where(odd, flux_one, flux_up).astype(bf16)

    q_top = x_ref[pl.ds(ROWS - 1, FEAT, stride=ROWS), :]
    q_under = x_ref[pl.ds(ROWS - 2, FEAT, stride=ROWS), :]
    top = slice(ROWS - 1, ROWS)
    after_top = (
        keep[top] * q_top + west[top] * pltpu.roll(q_top, 1, 1) + south[top] * q_under
    )
    north_out_ref[0:FEAT, :] = (north[top] * q_top).astype(bf16)
    north_out_ref[FPAD : FPAD + FEAT, :] = (north[top] * after_top).astype(bf16)
    pad = jnp.broadcast_to(north[top], (FPAD - FEAT, COLS)).astype(bf16)
    north_out_ref[FEAT:FPAD, :] = pad
    north_out_ref[FPAD + FEAT :, :] = pad


def transport_kernel(
    table_ref, x_hbm, east_ref, north_ref, rim_ref, south_ref, corner_ref,
    field_hbm, own_hbm, send_hbm,
    x_ref, field_ref, inflow_ref, rims_ref, south32_ref, own_ref, send_ref, sems,
):
    x_in = [
        pltpu.make_async_copy(
            x_hbm.at[pl.ds(a, b - a)], x_ref.at[pl.ds(a, b - a)], sems.at[1 + ROWS + ROWS // 2 + i]
        )
        for i, (a, b) in enumerate(zip(X_CUTS[:-1], X_CUTS[1:]))
    ]
    for copy in x_in:
        copy.start()
    x_ref[FLAT:, :] = jnp.zeros((x_ref.shape[0] - FLAT, COLS), f32)
    field_ref[:, GROUPS * 8 :, :] = jnp.zeros((ROWS, FPAD - GROUPS * 8, COLS), f32)
    south32_ref[...] = south_ref[...].astype(f32)
    to_slot = table_ref[0, 3]
    is_dyn = to_slot == 1
    east, north, keep, west, south = coefficients(
        east_ref[...], north_ref[...], to_slot.astype(f32), table_ref[0, 2].astype(f32)
    )
    keep, west, south = (value.reshape(ROWS, 1, COLS) for value in (keep, west, south))
    lane = lane_ids((128, COLS))
    rim = rim_ref[...].astype(f32)
    corner = pltpu.roll(corner_ref[...].astype(f32), 128 - (ROWS - 1), 0)
    east_courant = rim[0:1, COLS - 1 : COLS]
    north_courant = south32_ref[FEAT : FEAT + 1, 0:1]
    lacked = corner * east_courant + pltpu.roll(corner, COLS - 1, 1) * north_courant
    fix = jnp.logical_and(row_ids((128, COLS)) % ROWS == 0, lane % 2 == 0)
    inflow_ref[...] = rim + jnp.where(fix, lacked, 0.0)
    for k in range(ROWS):
        rims_ref[k] = inflow_ref[pl.ds(k, 8, stride=ROWS), :]
    both = rims_ref[...]
    one = pltpu.roll(both, COLS - 1, 2)
    below = jnp.concatenate([one[ROWS - 1 :], one[: ROWS - 1]], axis=0)
    rims_ref[...] = jnp.where(
        lane_ids((ROWS, 8, COLS)) % 2 == 1,
        west[:, :, 1:2] * both,
        both + keep[:, :, 0:1] * one + south[:, :, 0:1] * below,
    )
    reached = lane_ids((ROWS, 8, COLS)) < 2

    def transported(q, from_south):
        under = jnp.concatenate([q[ROWS - 1 :], q[: ROWS - 1]], axis=0)
        after = keep * q + west * pltpu.roll(q, 1, 2) + south * under
        return jnp.concatenate([after[:1] + from_south[None], after[1:]], axis=0)

    def group(g, carry):
        features = pl.ds(pl.multiple_of(g * 8, 8), 8)
        over = pl.ds(pl.multiple_of(FPAD + g * 8, 8), 8)
        q = jnp.stack([x_ref[pl.ds(g * 128 + k, 8, stride=ROWS), :] for k in range(ROWS)])
        q = transported(q, south32_ref[features, :])
        q = transported(q, south32_ref[over, :])
        inflow = pltpu.roll(rims_ref[...], lax.rem(COLS - 2 * g, COLS), 2)
        field_ref[:, features, :] = q + jnp.where(reached, inflow, 0.0)
        return carry

    field_out = []
    n_cuts = len(x_in)
    for i, copy in enumerate(x_in):
        copy.wait()
        first, end = 8 * i, min(8 * i + 8, GROUPS)
        lax.fori_loop(first, end, group, 0, unroll=4 if end - first == 8 else True)
        part = pl.ds(8 * first, 8 * (end - first) if end < GROUPS else FPAD - 8 * first)
        field_out.append(
            pltpu.make_async_copy(
                field_ref.at[:, part], field_hbm.at[:, part], sems.at[1 + ROWS + ROWS // 2 + n_cuts + i]
            )
        )
        field_out[-1].start()

    low = lane_ids((PACK, COLS)) < COLS // 2
    low_full = lane_ids((FPAD, COLS)) < COLS // 2

    def pair_body(i, carry):
        kept = []
        for side in range(2):
            r = 2 * i + side
            here = field_ref[table_ref[r, 0]]
            turned = pltpu.roll(here, COLS // 2, 1)
            value = jnp.where(is_dyn, here, turned)
            other = jnp.where(is_dyn, turned, here)
            packed = jnp.where(low, other[:PACK], value[PACK:])
            send_ref[r] = packed.astype(bf16)
            pltpu.make_async_copy(
                send_ref.at[r], send_hbm.at[2 * r + to_slot], sems.at[1 + r]
            ).start()
            kept.append(value if side == 0 else other)
        own_ref[i] = jnp.where(low_full, kept[0], kept[1]).astype(bf16)
        pltpu.make_async_copy(own_ref.at[i], own_hbm.at[i], sems.at[1 + ROWS + i]).start()
        return carry

    lax.fori_loop(0, ROWS // 2, pair_body, 0, unroll=2)
    for copy in field_out:
        copy.wait()
    for r in range(ROWS):
        pltpu.make_async_copy(
            send_ref.at[r], send_hbm.at[2 * r + to_slot], sems.at[1 + r]
        ).wait()
    for i in range(ROWS // 2):
        pltpu.make_async_copy(own_ref.at[i], own_hbm.at[i], sems.at[1 + ROWS + i]).wait()


def sigmoid(value):
    return 0.5 + 0.5 * jnp.tanh(0.5 * value)


def swap_halves(value):
    return pltpu.roll(value, COLS // 2, 1)


def forward_kernel(
    table_ref, own_ref, recv_ref, w_one_ref, w_two_ref, w_three_ref, gain_ref,
    inputs_ref, hidden_ref, g_two_ref, slope_ref, own_out_ref, send_ref, vec_ref,
):
    from_slot = table_ref[0, 3]
    offset = table_ref[0, 4]
    low = lane_ids((PACK, COLS)) < COLS // 2
    gain = gain_ref[...]
    loss_norm = 1.0 / math.sqrt(ROWS * 8 * COLS * ROWS)
    energy_norm = 1.0 / math.sqrt(OUT)
    tile = MINE
    vec_ref[...] = jnp.zeros(vec_ref.shape, f32)

    lanes = slice(0, MINE)
    live_parts = []
    for i in range(ROWS // 2):
        group = slice(i * COLS, (i + 1) * COLS)
        first = recv_ref[4 * i + from_slot].astype(f32)
        second = recv_ref[4 * i + 2 + from_slot].astype(f32)
        inputs_ref[0:FPAD, group] = own_ref[i]
        inputs_ref[FPAD : FPAD + PACK, group] = jnp.where(
            low, first, swap_halves(second)
        ).astype(bf16)
        inputs_ref[FPAD + PACK :, group] = jnp.where(
            low, swap_halves(first), second
        ).astype(bf16)
        lane = lane_ids((1, COLS))
        column = lane % (COLS // 2) + offset
        cost = jnp.where(lane < COLS // 2, table_ref[2 * i, 1], table_ref[2 * i + 1, 1])
        live_parts.append(jnp.where(column < cost, 1.0, 0.0))
    live = jnp.concatenate(live_parts, axis=1)
    inputs = inputs_ref[:, lanes]
    pre_one = jnp.dot(w_one_ref[...], inputs, preferred_element_type=f32)
    sig = sigmoid(pre_one)
    silu = pre_one * sig
    hidden_one = silu.astype(bf16)
    slope_ref[:, lanes] = sig + silu * (1.0 - sig)
    hidden_ref[:, lanes] = hidden_one
    pre_two = jnp.dot(w_two_ref[...], hidden_one, preferred_element_type=f32)
    sig = sigmoid(pre_two)
    silu = pre_two * sig
    hidden_two = silu.astype(bf16)
    slope_two = sig + silu * (1.0 - sig)
    result = jnp.dot(w_three_ref[...], hidden_two, preferred_element_type=f32).astype(bf16)
    own_out_ref[:, lanes] = result[:FPAD]
    to_send = result[FPAD:].astype(f32)
    for i in range(ROWS // 2):
        part = to_send[:, i * COLS : (i + 1) * COLS]
        other = swap_halves(part)
        zeros = jnp.zeros((PACK, COLS), bf16)
        send_ref[4 * i + from_slot] = jnp.where(low, part[:PACK], other[PACK:]).astype(bf16)
        send_ref[4 * i + 2 + from_slot] = jnp.where(
            low, other[:PACK], part[PACK:]
        ).astype(bf16)
        send_ref[4 * i + 1 - from_slot] = zeros
        send_ref[4 * i + 3 - from_slot] = zeros
    energy = jnp.sum(gain * hidden_two.astype(f32), axis=0, keepdims=True) * energy_norm
    weight = live * energy * loss_norm
    g_two_ref[:, lanes] = (gain * weight * slope_two).astype(bf16)
    high = weight.astype(bf16)
    left = weight - high.astype(f32)
    mid = left.astype(bf16)
    low_part = (left - mid.astype(f32)).astype(bf16)
    rows = row_ids((16, tile))
    stacked = jnp.where(
        rows == 0,
        high.astype(f32),
        jnp.where(rows == 1, mid.astype(f32), jnp.where(rows == 2, low_part.astype(f32), 0.0)),
    ).astype(bf16)
    vec_ref[...] += lax.dot_general(stacked, hidden_two, NT, preferred_element_type=f32)


def place(owner):
    core, x, za, zb, zc, y = (
        owner // 64, owner // 32 % 2, owner // 16 % 2, owner // 8 % 2, owner // 4 % 2, owner % 4
    )
    return core, zc * 32 + zb * 16 + za * 8 + y * 2 + x


def backward_kernel(
    table_ref, inputs_ref, hidden_ref, g_two_ref, slope_ref, w_mid_ref, vec_ref,
    keep_ref, send_ref, g_one_ref, d_in_ref,
):
    state_first = table_ref[0, 3]
    core = table_ref[0, 5]
    tile = 2 * COLS

    def tile_body(t, carry):
        lanes = pl.ds(pl.multiple_of(t * tile, tile), tile)
        back = jnp.dot(w_mid_ref[...], g_two_ref[:, lanes], preferred_element_type=f32)
        g_one_ref[:, lanes] = (back * slope_ref[:, lanes]).astype(bf16)
        return carry

    lax.fori_loop(0, MINE // tile, tile_body, 0, unroll=True)
    d_mid = lax.dot_general(hidden_ref[...], g_two_ref[...], NT, preferred_element_type=f32)
    g_one = g_one_ref[...]
    own_at = pl.multiple_of((1 - state_first) * FPAD, 8)
    recv_at = pl.multiple_of(state_first * FPAD, 8)
    d_in_ref[pl.ds(own_at, FPAD), :] = lax.dot_general(
        inputs_ref[:FPAD, :], g_one, NT, preferred_element_type=f32
    )
    d_in_ref[pl.ds(recv_at, FPAD), :] = lax.dot_general(
        inputs_ref[FPAD:, :], g_one, NT, preferred_element_type=f32
    )

    def write(refs):
        def put(owner, at, value):
            half, index = place(owner)
            refs[half][index, at : at + 8, :] = value

        def put_a(row, value):
            put(row // A_PIECE, row % A_PIECE, value)

        def put_b(row, value):
            put(row // B_PIECE, A_PIECE, value)

        for l in range(3):
            lanes = slice(l * 128, (l + 1) * 128)
            for k in range(2 * FPAD // 8):
                put_a(l * A_ROWS + k * 8, d_in_ref[k * 8 : k * 8 + 8, lanes])
            for k in range((A_ROWS - 2 * FPAD) // 8):
                put_a(l * A_ROWS + 2 * FPAD + k * 8, d_mid[k * 8 : k * 8 + 8, lanes])
            for k in range(B_ROWS // 8):
                put_b(l * B_ROWS + k * 8, d_mid[96 + k * 8 : 96 + k * 8 + 8, lanes])
        zeros = jnp.zeros((8, 128), f32)
        for row in range(3 * A_ROWS, OWNERS * A_PIECE, 8):
            put_a(row, zeros)
        vec = jnp.sum(vec_ref[...], axis=0, keepdims=True)
        for l in range(3):
            put_b(3 * B_ROWS + l * 8, jnp.broadcast_to(vec[:, l * 128 : (l + 1) * 128], (8, 128)))
        for row in range(3 * B_ROWS + 24, OWNERS * B_PIECE, 8):
            put_b(row, zeros)

    @pl.when(core == 0)
    def _():
        write((keep_ref, send_ref))

    @pl.when(core == 1)
    def _():
        write((send_ref, keep_ref))


def final_kernel(table_ref, field_ref, own_ref, recv_ref, out_ref, new_ref):
    from_slot = table_ref[0, 3]
    is_dyn = from_slot == 1
    keep_scale = jnp.where(is_dyn, 1.0, 0.0)
    new_scale = jnp.where(is_dyn, 0.5, 1.0)
    low_full = lane_ids((FPAD, COLS)) < COLS // 2

    def pair_body(i, carry):
        pair = own_ref[:, pl.ds(pl.multiple_of(i * COLS, COLS), COLS)].astype(f32)
        for side in range(2):
            r = 2 * i + side
            chunk = recv_ref[2 * r + from_slot].astype(f32)
            theirs = jnp.concatenate([swap_halves(chunk), chunk], axis=0)
            mine = pair if side == 0 else swap_halves(pair)
            tend = jnp.where(low_full, mine, theirs)
            tend = jnp.where(is_dyn, tend, swap_halves(tend))
            old = field_ref[table_ref[r, 0]]
            live = lane_ids((FPAD, COLS)) < table_ref[r, 1]
            new_ref[table_ref[r, 0]] = jnp.where(live, keep_scale * old + new_scale * tend, old)
        return carry

    lax.fori_loop(0, ROWS // 2, pair_body, 0, unroll=2)
    full, rest = chunks()

    def group(g, carry):
        value = jnp.swapaxes(new_ref[:, pl.ds(pl.multiple_of(g * 8, 8), 8), :], 0, 1)
        out_ref[pl.ds(pl.multiple_of(g * 128, 128), 128), :] = value.reshape(128, COLS)
        return carry

    lax.fori_loop(0, full, group, 0, unroll=2)
    value = jnp.swapaxes(new_ref[:, full * 8 : full * 8 + 8, :], 0, 1).reshape(128, COLS)
    out_ref[full * 128 :, :] = value[: rest * ROWS]


MID_A = 98
PERIOD = 23
OUT_AT = 3 * (HID - MID_A)


def gather_kernel(
    table_ref, mine_ref, x_other_ref, core_other_ref, far_ref, energy_ref, out_ref, all_ref, vec_ref
):
    is_dyn = table_ref[0, 3] == 1
    core = table_ref[0, 5]
    x = table_ref[0, 6]
    all_ref[2 * core + x] = mine_ref[...]
    all_ref[2 * core + 1 - x] = x_other_ref[...]
    all_ref[2 * (1 - core) + x] = core_other_ref[...]
    all_ref[2 * (1 - core) + 1 - x] = far_ref[...]

    def rows_at(row, count):
        quarter = OWNERS // 4 * A_PIECE
        parts = []
        while count:
            here = min(count, quarter - row % quarter)
            parts.append(all_ref[row // quarter, row % quarter : row % quarter + here, :])
            row, count = row + here, count - here
        return parts[0] if len(parts) == 1 else jnp.concatenate(parts, axis=0)

    @pl.when(is_dyn)
    def _():
        for l in range(3):
            for first, source, count in ((0, 0, FEAT), (FEAT, FPAD, FEAT), (2 * FEAT, 2 * FPAD, MID_A)):
                out_ref[pl.ds(3 * first + l, count, stride=3), :] = rows_at(
                    l * A_ROWS + source, count
                )

    @pl.when(jnp.logical_not(is_dyn))
    def _():
        skip = MID_A - 96
        for l in range(3):
            for m in range(B_ROWS // 8):
                value = rows_at((l * B_ROWS // 8 + m) * A_PIECE, 8)
                value = value[skip:] if m == 0 else value
                first = 0 if m == 0 else 8 * m - skip
                out_ref[pl.ds(3 * first + l, value.shape[0], stride=3), :] = value
        for l in range(3):
            value = rows_at((3 * B_ROWS // 8 + l) * A_PIECE, 8)
            value = jnp.concatenate([value] * 16, axis=0)
            vec_ref[l * 128 : (l + 1) * 128, :] = value.T
        vec_ref[HID:, :] = jnp.zeros((8, 128), f32)
        lane = lane_ids((HID // 8, 128))
        for k in range(PERIOD):
            h, start = 128 * k // OUT, 128 * k
            bound = OUT * (h + 1) - start
            value = vec_ref[pl.ds(h, HID // 8, stride=8), :]
            if bound < 128:
                after = vec_ref[pl.ds(h + 1, HID // 8, stride=8), :]
                value = jnp.where(lane < bound, value, after)
            out_ref[pl.ds(OUT_AT + k, HID // 8, stride=PERIOD), :] = value * energy_ref[k : k + 1, :]


def shape(dims, dtype):
    return jax.ShapeDtypeStruct(dims, dtype)


def swap(value, axis):
    return lax.ppermute(value, axis, [(0, 1), (1, 0)])


def on_device(columns, east_courant, north_courant, assign, block_cost, w_in, w_mid, w_out, energy):
    bands = lax.axis_size(LAT)
    lons = lax.axis_size(LON)
    is_physics = lax.axis_index("grp") == 1
    stored = columns.reshape(FLAT, COLS)

    n_copies = len(X_CUTS) - 1 + 4
    rim, corner, north_out, table = vmem_call(
        rim_kernel,
        [
            shape((128, COLS), bf16),
            shape((128, COLS), bf16),
            shape((2 * FPAD, COLS), bf16),
            shape((ROWS, COLS), jnp.int32),
        ],
        [
            pltpu.VMEM((FLAT, COLS), f32),
            pltpu.VMEM((ROWS, COLS), f32),
            pltpu.VMEM((ROWS, COLS), f32),
            pltpu.VMEM((ROWS, ROWS), jnp.int32),
            pltpu.VMEM((ROWS, ROWS), jnp.int32),
            pltpu.SemaphoreType.DMA((n_copies,)),
        ],
        "hhhhh",
        10**8,
        3 * 10**6,
        "rim",
        ALL_VMEM,
    )(stored, east_courant, north_courant, assign, block_cost)
    from_west = lax.ppermute(rim, LON, [(i, (i + 1) % lons) for i in range(lons)])
    from_south = lax.ppermute(north_out, LAT, [(i, i + 1) for i in range(bands - 1)])
    from_corner = lax.ppermute(
        corner,
        LAT + LON,
        [(b * lons + i, (b + 1) * lons + (i + 1) % lons) for b in range(bands - 1) for i in range(lons)],
    )

    def halves(a, b, axis):
        first = jnp.where(is_physics, b, a)
        second = jnp.where(is_physics, a, b)
        pad = [(0, 0), (0, 0)]
        pad[axis] = (0, FPAD - FEAT)
        return jnp.concatenate([jnp.pad(first, pad), jnp.pad(second, pad)], axis=axis)

    w_in_t = w_in.T
    w_one = halves(w_in_t[:, :FEAT], w_in_t[:, FEAT:], 1)
    w_out_t = w_out.T
    w_three = halves(w_out_t[:FEAT], w_out_t[OUT - FEAT :], 0)
    gain = jnp.sum(w_out.astype(f32) * energy[None, :], axis=1, keepdims=True)

    field, own, send = vmem_call(
        transport_kernel,
        [
            shape((ROWS, FPAD, COLS), f32),
            shape((ROWS // 2, FPAD, COLS), bf16),
            shape((2 * ROWS, PACK, COLS), bf16),
        ],
        [
            pltpu.VMEM((GROUPS * 128, COLS), f32),
            pltpu.VMEM((ROWS, FPAD, COLS), f32),
            pltpu.VMEM((128, COLS), f32),
            pltpu.VMEM((ROWS, 8, COLS), f32),
            pltpu.VMEM((2 * FPAD, COLS), f32),
            pltpu.VMEM((ROWS // 2, FPAD, COLS), bf16),
            pltpu.VMEM((ROWS, PACK, COLS), bf16),
            pltpu.SemaphoreType.DMA((1 + ROWS + ROWS // 2 + 2 * (len(X_CUTS) - 1),)),
        ],
        "shvvvvv",
        10**8,
        6 * 10**6,
        "transport",
        ALL_VMEM,
        "hhh",
    )(table, stored, east_courant, north_courant, from_west, from_south, from_corner)
    recv = lax.all_to_all(send, LON + ("grp",), 0, 0, tiled=True)
    inputs, hidden, g_two, slope, own_out, send_back, vec = vmem_call(
        forward_kernel,
        [
            shape((2 * FPAD, MINE), bf16),
            shape((HID, MINE), bf16),
            shape((HID, MINE), bf16),
            shape((HID, MINE), f32),
            shape((FPAD, MINE), bf16),
            shape((2 * ROWS, PACK, COLS), bf16),
            shape((16, HID), f32),
        ],
        [],
        "svvvvvv",
        2 * MINE * HID * (4 * FPAD + HID),
        8 * 10**6,
        "forward",
        16,
    )(table, own, recv, w_one, w_mid.T, w_three, gain)
    back = lax.all_to_all(send_back, LON + ("grp",), 0, 0, tiled=True)
    keep, other = vmem_call(
        backward_kernel,
        [shape((OWNERS // 2, PIECE, 128), f32)] * 2,
        [pltpu.VMEM((HID, MINE), bf16), pltpu.VMEM((2 * FPAD, HID), f32)],
        "svvvvvv",
        2 * MINE * HID * (2 * FPAD + 2 * HID),
        6 * 10**6,
        "backward",
        16,
    )(table, inputs, hidden, g_two, slope, w_mid, vec)

    grad = keep + swap(other, "core")
    for axis in ("zc", "zb"):
        pieces = grad.shape[0] // 2
        at = lax.axis_index(axis)
        other = lax.dynamic_slice_in_dim(grad, (1 - at) * pieces, pieces)
        keep = lax.dynamic_slice_in_dim(grad, at * pieces, pieces)
        grad = keep + swap(other.astype(bf16), axis).astype(f32)
    grad, back = lax.optimization_barrier((grad, back))
    pieces_b = jnp.pad(grad[:, A_PIECE:], ((0, 0), (0, A_PIECE - B_PIECE), (0, 0)))
    pieces = jnp.stack([grad[:, :A_PIECE], pieces_b], axis=1).reshape(-1, A_PIECE, 128)
    piece = jnp.sum(lax.all_to_all(pieces, ("za", "y", "x", "grp"), 0, 0, tiled=True), axis=0)
    ring = LAT + ("y",)
    members = bands * lax.axis_size("y")
    piece = lax.all_to_all(
        jnp.broadcast_to(piece[None], (members,) + piece.shape), ring, 0, 0, tiled=True
    )
    new = vmem_call(
        final_kernel,
        [shape((FLAT, COLS), f32)],
        [pltpu.VMEM((ROWS, FPAD, COLS), f32)],
        "svvv",
        10**7,
        6 * 10**6,
        "final",
        16,
    )(table, field, own_out, back)[0]
    core_other = swap(piece, "core")
    x_other = swap(piece, "x")
    x_other, new = lax.optimization_barrier((x_other, new))
    far = swap(x_other, "core")
    energy_rows = jnp.tile(energy, 8).reshape(PERIOD, 128)
    quarter = (OWNERS // 4 * A_PIECE, 128)
    grad_half = vmem_call(
        gather_kernel,
        [shape((3 * (2 * FEAT + MID_A), 128), f32)],
        [pltpu.VMEM((4,) + quarter, f32), pltpu.VMEM((HID + 8, 128), f32)],
        "svvvvv",
        10**7,
        2 * 10**6,
        "gather",
        16,
    )(table, *(value.reshape(quarter) for value in (piece, x_other, core_other, far)), energy_rows)[0]
    return new.reshape(columns.shape), grad_half.reshape(-1)


def solution(mesh):
    lat, lon, grp = mesh.devices.shape
    split = Mesh(mesh.devices.reshape(lat // 4, 2, 2, lon // 4, 2, 2, grp), LAT + LON + ("grp",))
    grid = P(LAT, LON)
    columns = P("grp", None, LAT, LON)
    return jax.shard_map(
        on_device,
        mesh=split,
        in_specs=(columns, grid, grid, P(), P(), P(), P(), P(), P()),
        out_specs=(columns, P("grp")),
        check_vma=False,
    )
```

```python
import functools
import math

import jax
import jax.numpy as jnp
from jax import lax
from jax.experimental import pallas as pl
from jax.experimental.pallas import tpu as pltpu
from jax.sharding import Mesh, PartitionSpec as P

f32 = jnp.float32
bf16 = jnp.bfloat16

FEAT = 278
FPAD = 288
PACK = 144
ROWS = 16
COLS = 128
HID = 384
OUT = 368
FLAT = FEAT * ROWS
MINE = ROWS * COLS // 2
LON = ("y", "x", "core")
LAT = ("za", "zb", "zc")
MIB = 1024 * 1024
ALL_VMEM = 60

NT = (((1,), (1,)), ((), ()))
TN = (((0,), (0,)), ((), ()))

A_ROWS = 680
B_ROWS = 288
OWNERS = 128
A_PIECE = 16
B_PIECE = 8
PIECE = A_PIECE + B_PIECE


def vmem_call(kernel, outs, scratch, places, flops, size, name, limit, out_places=None):
    spaces = {"s": pltpu.SMEM, "v": pltpu.VMEM, "h": pltpu.HBM}
    out_places = out_places or "v" * len(outs)
    return pl.pallas_call(
        kernel,
        out_shape=outs,
        in_specs=[pl.BlockSpec(memory_space=spaces[p]) for p in places],
        out_specs=[pl.BlockSpec(memory_space=spaces[p]) for p in out_places],
        scratch_shapes=scratch,
        compiler_params=pltpu.CompilerParams(vmem_limit_bytes=limit * MIB),
        cost_estimate=pl.CostEstimate(flops=flops, bytes_accessed=size, transcendentals=0),
        name=name,
    )


def lane_ids(shape):
    return lax.broadcasted_iota(jnp.int32, shape, len(shape) - 1)


def row_ids(shape):
    return lax.broadcasted_iota(jnp.int32, shape, len(shape) - 2)


def chunks():
    full = FEAT // 8
    return full, FEAT - full * 8


def coefficients(east, north, dyn, not_top):
    rows = row_ids(north.shape)
    north = jnp.where(rows == ROWS - 1, north * not_top, north) * dyn
    east = east * dyn
    keep = 1.0 - east - north
    west = jnp.where(lane_ids(east.shape) == 0, 0.0, pltpu.roll(east, 1, 1))
    south = jnp.where(rows == 0, 0.0, pltpu.roll(north, 1, 0))
    return east, north, keep, west, south


def tiled_column(value, lane):
    column = jnp.broadcast_to(value[:, lane : lane + 1], (ROWS, COLS))
    return jnp.concatenate([column] * 8, axis=0)


def block_table(is_physics, lon, facts, targets, costs, own_targets, own_costs):
    ids = lax.broadcasted_iota(jnp.int32, (ROWS, ROWS), 0)
    ks = lax.broadcasted_iota(jnp.int32, (ROWS, ROWS), 1)
    own_targets = jnp.broadcast_to(own_targets, (ROWS, ROWS))
    own_costs = jnp.broadcast_to(own_costs, (ROWS, ROWS))
    at_home = own_targets // ROWS == ids
    at_slot = targets // ROWS == lon
    rows = jnp.where(
        is_physics, jnp.where(at_slot, targets % ROWS, 0), jnp.where(at_home, ks, 0)
    )
    costs = jnp.where(is_physics, jnp.where(at_slot, costs, 0), jnp.where(at_home, own_costs, 0))
    rows = jnp.sum(rows, axis=1, keepdims=True)
    costs = jnp.sum(costs, axis=1, keepdims=True)
    lane = lane_ids((ROWS, COLS))
    table = jnp.where(lane == 0, rows, jnp.where(lane == 1, costs, 0))
    for k, fact in enumerate(facts):
        table = jnp.where(lane == 2 + k, fact, table)
    return table


GROUPS = -(-FEAT // 8)
X_CUTS = tuple(range(0, FLAT, 1024)) + (FLAT,)


def rim_kernel(
    x_hbm, east_hbm, north_hbm, assign_hbm, cost_hbm,
    rim_ref, corner_ref, north_out_ref, table_ref,
    x_ref, east_ref, north_ref, assign_ref, cost_ref, sems,
):
    band = lax.axis_index(LAT)
    lon = lax.axis_index(LON)
    grp = lax.axis_index("grp")
    core = lax.axis_index("core")
    not_top = jnp.where(band != lax.axis_size(LAT) - 1, 1, 0)
    copies = [
        pltpu.make_async_copy(x_hbm.at[pl.ds(a, b - a)], x_ref.at[pl.ds(a, b - a)], sems.at[i])
        for i, (a, b) in enumerate(zip(X_CUTS[:-1], X_CUTS[1:]))
    ]
    n = len(copies)
    small = [
        pltpu.make_async_copy(east_hbm, east_ref, sems.at[n]),
        pltpu.make_async_copy(north_hbm, north_ref, sems.at[n + 1]),
        pltpu.make_async_copy(assign_hbm.at[band], assign_ref, sems.at[n + 2]),
        pltpu.make_async_copy(cost_hbm.at[band], cost_ref, sems.at[n + 3]),
    ]
    for copy in small + copies:
        copy.start()
    for copy in small:
        copy.wait()
    table_ref[...] = block_table(
        grp == 1,
        lon,
        (not_top, 1 - grp, grp * (COLS // 2), core, lax.axis_index("x")),
        assign_ref[...],
        cost_ref[...],
        assign_ref[pl.ds(lon, 1), :],
        cost_ref[pl.ds(lon, 1), :],
    )
    east, north, keep, west, south = coefficients(
        east_ref[...], north_ref[...], (1 - grp).astype(f32), not_top.astype(f32)
    )
    full, rest = chunks()
    lane = lane_ids((128, COLS))
    picked = jnp.zeros((128, COLS), f32)
    for g in range(full):
        if g % 8 == 0:
            copies[g // 8].wait()
        turned = pltpu.roll(x_ref[g * 128 : (g + 1) * 128, :], 2 * g + 2, 1)
        picked = jnp.where(lane // 2 == g, turned, picked)
    tail = pltpu.roll(x_ref[full * 128 :, :], 2 * full + 2, 1)
    tail = jnp.concatenate([tail, jnp.zeros((128 - rest * ROWS, COLS), f32)], axis=0)
    picked = jnp.where(lane // 2 == full, tail, picked)

    last = COLS - 1
    east_last = tiled_column(east, last)
    after = (
        tiled_column(keep, last) * picked
        + tiled_column(west, last) * pltpu.roll(picked, 1, 1)
        + tiled_column(south, last) * pltpu.roll(picked, 1, 0)
    )
    odd = lane % 2 == 1
    flux_one = east_last * picked
    flux_two = pltpu.roll(east_last * after, COLS - 1, 1)
    flux_up = pltpu.roll(tiled_column(north, last) * picked, COLS - 1, 1)
    scalar = jnp.broadcast_to(east[0:1, last:], (128, COLS))
    rim = jnp.where(odd, flux_one, flux_two)
    rim_ref[...] = jnp.where(lane == last, scalar, rim).astype(bf16)
    corner_ref[...] = jnp.where(odd, flux_one, flux_up).astype(bf16)

    q_top = x_ref[pl.ds(ROWS - 1, FEAT, stride=ROWS), :]
    q_under = x_ref[pl.ds(ROWS - 2, FEAT, stride=ROWS), :]
    top = slice(ROWS - 1, ROWS)
    after_top = (
        keep[top] * q_top + west[top] * pltpu.roll(q_top, 1, 1) + south[top] * q_under
    )
    pad = jnp.broadcast_to(north[top], (FPAD - FEAT, COLS))
    for at, flux in ((0, north[top] * q_top), (FPAD, north[top] * after_top)):
        north_out_ref[at : at + FPAD, :] = jnp.concatenate([flux, pad], axis=0).astype(bf16)


def transport_kernel(
    table_ref, x_hbm, east_ref, north_ref, rim_ref, south_ref, corner_ref,
    field_hbm, own_hbm, send_hbm,
    x_ref, field_ref, inflow_ref, rims_ref, south32_ref, own_ref, send_ref, sems,
):
    x_in = [
        pltpu.make_async_copy(
            x_hbm.at[pl.ds(a, b - a)], x_ref.at[pl.ds(a, b - a)], sems.at[1 + ROWS + ROWS // 2 + i]
        )
        for i, (a, b) in enumerate(zip(X_CUTS[:-1], X_CUTS[1:]))
    ]
    for copy in x_in:
        copy.start()
    x_ref[FLAT:, :] = jnp.zeros((x_ref.shape[0] - FLAT, COLS), f32)
    field_ref[:, GROUPS * 8 :, :] = jnp.zeros((ROWS, FPAD - GROUPS * 8, COLS), f32)
    south32_ref[...] = south_ref[...].astype(f32)
    to_slot = table_ref[0, 3]
    is_dyn = to_slot == 1
    east, north, keep, west, south = coefficients(
        east_ref[...], north_ref[...], to_slot.astype(f32), table_ref[0, 2].astype(f32)
    )
    keep, west, south = (value.reshape(ROWS, 1, COLS) for value in (keep, west, south))
    lane = lane_ids((128, COLS))
    rim = rim_ref[...].astype(f32)
    corner = pltpu.roll(corner_ref[...].astype(f32), 128 - (ROWS - 1), 0)
    east_courant = rim[0:1, COLS - 1 : COLS]
    north_courant = south32_ref[FEAT : FEAT + 1, 0:1]
    lacked = corner * east_courant + pltpu.roll(corner, COLS - 1, 1) * north_courant
    fix = jnp.logical_and(row_ids((128, COLS)) % ROWS == 0, lane % 2 == 0)
    inflow_ref[...] = rim + jnp.where(fix, lacked, 0.0)
    for k in range(ROWS):
        rims_ref[k] = inflow_ref[pl.ds(k, 8, stride=ROWS), :]
    both = rims_ref[...]
    one = pltpu.roll(both, COLS - 1, 2)
    below = jnp.concatenate([one[ROWS - 1 :], one[: ROWS - 1]], axis=0)
    rims_ref[...] = jnp.where(
        lane_ids((ROWS, 8, COLS)) % 2 == 1,
        west[:, :, 1:2] * both,
        both + keep[:, :, 0:1] * one + south[:, :, 0:1] * below,
    )
    reached = lane_ids((ROWS, 8, COLS)) < 2

    def transported(q, from_south):
        under = jnp.concatenate([q[ROWS - 1 :], q[: ROWS - 1]], axis=0)
        after = keep * q + west * pltpu.roll(q, 1, 2) + south * under
        return jnp.concatenate([after[:1] + from_south[None], after[1:]], axis=0)

    def group(g, carry):
        features = pl.ds(pl.multiple_of(g * 8, 8), 8)
        over = pl.ds(pl.multiple_of(FPAD + g * 8, 8), 8)
        q = jnp.stack([x_ref[pl.ds(g * 128 + k, 8, stride=ROWS), :] for k in range(ROWS)])
        q = transported(q, south32_ref[features, :])
        q = transported(q, south32_ref[over, :])
        inflow = pltpu.roll(rims_ref[...], lax.rem(COLS - 2 * g, COLS), 2)
        field_ref[:, features, :] = q + jnp.where(reached, inflow, 0.0)
        return carry

    field_out = []
    n_cuts = len(x_in)
    for i, copy in enumerate(x_in):
        copy.wait()
        first, end = 8 * i, min(8 * i + 8, GROUPS)
        lax.fori_loop(first, end, group, 0, unroll=True)
        part = pl.ds(8 * first, 8 * (end - first) if end < GROUPS else FPAD - 8 * first)
        field_out.append(
            pltpu.make_async_copy(
                field_ref.at[:, part], field_hbm.at[:, part], sems.at[1 + ROWS + ROWS // 2 + n_cuts + i]
            )
        )
        field_out[-1].start()

    low = lane_ids((PACK, COLS)) < COLS // 2
    low_full = lane_ids((FPAD, COLS)) < COLS // 2

    def pair_body(i, carry):
        kept = []
        for side in range(2):
            r = 2 * i + side
            here = field_ref[table_ref[r, 0]]
            turned = pltpu.roll(here, COLS // 2, 1)
            value = jnp.where(is_dyn, here, turned)
            other = jnp.where(is_dyn, turned, here)
            packed = jnp.where(low, other[:PACK], value[PACK:])
            send_ref[r] = packed.astype(bf16)
            pltpu.make_async_copy(
                send_ref.at[r], send_hbm.at[2 * r + to_slot], sems.at[1 + r]
            ).start()
            kept.append(value if side == 0 else other)
        own_ref[i] = jnp.where(low_full, kept[0], kept[1]).astype(bf16)
        pltpu.make_async_copy(own_ref.at[i], own_hbm.at[i], sems.at[1 + ROWS + i]).start()
        return carry

    lax.fori_loop(0, ROWS // 2, pair_body, 0, unroll=2)
    for copy in field_out:
        copy.wait()
    for r in range(ROWS):
        pltpu.make_async_copy(
            send_ref.at[r], send_hbm.at[2 * r + to_slot], sems.at[1 + r]
        ).wait()
    for i in range(ROWS // 2):
        pltpu.make_async_copy(own_ref.at[i], own_hbm.at[i], sems.at[1 + ROWS + i]).wait()


def sigmoid(value):
    return 0.5 + 0.5 * jnp.tanh(0.5 * value)


def swap_halves(value):
    return pltpu.roll(value, COLS // 2, 1)


def forward_kernel(
    table_ref, own_ref, recv_ref, w_one_ref, w_two_ref, w_three_ref, gain_ref,
    inputs_ref, hidden_ref, g_two_ref, slope_ref, own_out_ref, send_ref, vec_ref,
):
    from_slot = table_ref[0, 3]
    offset = table_ref[0, 4]
    low = lane_ids((PACK, COLS)) < COLS // 2
    gain = gain_ref[...]
    loss_norm = 1.0 / math.sqrt(ROWS * 8 * COLS * ROWS)
    energy_norm = 1.0 / math.sqrt(OUT)
    tile = MINE
    vec_ref[...] = jnp.zeros(vec_ref.shape, f32)

    lanes = slice(0, MINE)
    live_parts = []
    for i in range(ROWS // 2):
        group = slice(i * COLS, (i + 1) * COLS)
        first = recv_ref[4 * i + from_slot].astype(f32)
        second = recv_ref[4 * i + 2 + from_slot].astype(f32)
        inputs_ref[0:FPAD, group] = own_ref[i]
        inputs_ref[FPAD : FPAD + PACK, group] = jnp.where(
            low, first, swap_halves(second)
        ).astype(bf16)
        inputs_ref[FPAD + PACK :, group] = jnp.where(
            low, swap_halves(first), second
        ).astype(bf16)
        lane = lane_ids((1, COLS))
        column = lane % (COLS // 2) + offset
        cost = jnp.where(lane < COLS // 2, table_ref[2 * i, 1], table_ref[2 * i + 1, 1])
        live_parts.append(jnp.where(column < cost, 1.0, 0.0))
    live = jnp.concatenate(live_parts, axis=1)
    inputs = inputs_ref[:, lanes]
    pre_one = jnp.dot(w_one_ref[...], inputs, preferred_element_type=f32)
    sig = sigmoid(pre_one)
    silu = pre_one * sig
    hidden_one = silu.astype(bf16)
    slope_ref[:, lanes] = sig + silu * (1.0 - sig)
    hidden_ref[:, lanes] = hidden_one
    pre_two = jnp.dot(w_two_ref[...], hidden_one, preferred_element_type=f32)
    sig = sigmoid(pre_two)
    silu = pre_two * sig
    hidden_two = silu.astype(bf16)
    slope_two = sig + silu * (1.0 - sig)
    result = jnp.dot(w_three_ref[...], hidden_two, preferred_element_type=f32).astype(bf16)
    own_out_ref[:, lanes] = result[:FPAD]
    to_send = result[FPAD:].astype(f32)
    for i in range(ROWS // 2):
        part = to_send[:, i * COLS : (i + 1) * COLS]
        other = swap_halves(part)
        zeros = jnp.zeros((PACK, COLS), bf16)
        send_ref[4 * i + from_slot] = jnp.where(low, part[:PACK], other[PACK:]).astype(bf16)
        send_ref[4 * i + 2 + from_slot] = jnp.where(
            low, other[:PACK], part[PACK:]
        ).astype(bf16)
        send_ref[4 * i + 1 - from_slot] = zeros
        send_ref[4 * i + 3 - from_slot] = zeros
    energy = jnp.sum(gain * hidden_two.astype(f32), axis=0, keepdims=True) * energy_norm
    weight = live * energy * loss_norm
    g_two_ref[:, lanes] = (gain * weight * slope_two).astype(bf16)
    high = weight.astype(bf16)
    left = weight - high.astype(f32)
    mid = left.astype(bf16)
    low_part = (left - mid.astype(f32)).astype(bf16)
    rows = row_ids((16, tile))
    stacked = jnp.where(
        rows == 0,
        high.astype(f32),
        jnp.where(rows == 1, mid.astype(f32), jnp.where(rows == 2, low_part.astype(f32), 0.0)),
    ).astype(bf16)
    vec_ref[...] += lax.dot_general(stacked, hidden_two, NT, preferred_element_type=f32)


def place(owner):
    core, x, za, zb, zc, y = (
        owner // 64, owner // 32 % 2, owner // 16 % 2, owner // 8 % 2, owner // 4 % 2, owner % 4
    )
    return core, zc * 32 + zb * 16 + za * 8 + y * 2 + x


def backward_kernel(
    table_ref, inputs_ref, hidden_ref, g_two_ref, slope_ref, w_mid_ref, vec_ref,
    keep_ref, send_ref, g_one_ref, d_in_ref,
):
    state_first = table_ref[0, 3]
    core = table_ref[0, 5]
    tile = 2 * COLS

    def tile_body(t, carry):
        lanes = pl.ds(pl.multiple_of(t * tile, tile), tile)
        back = jnp.dot(w_mid_ref[...], g_two_ref[:, lanes], preferred_element_type=f32)
        g_one_ref[:, lanes] = (back * slope_ref[:, lanes]).astype(bf16)
        return carry

    lax.fori_loop(0, MINE // tile, tile_body, 0, unroll=True)
    d_mid = lax.dot_general(hidden_ref[...], g_two_ref[...], NT, preferred_element_type=f32)
    g_one = g_one_ref[...]
    own_at = pl.multiple_of((1 - state_first) * FPAD, 8)
    recv_at = pl.multiple_of(state_first * FPAD, 8)
    d_in_ref[pl.ds(own_at, FPAD), :] = lax.dot_general(
        inputs_ref[:FPAD, :], g_one, NT, preferred_element_type=f32
    )
    d_in_ref[pl.ds(recv_at, FPAD), :] = lax.dot_general(
        inputs_ref[FPAD:, :], g_one, NT, preferred_element_type=f32
    )

    def write(refs):
        def put(owner, at, value):
            half, index = place(owner)
            refs[half][index, at : at + 8, :] = value

        def put_a(row, value):
            put(row // A_PIECE, row % A_PIECE, value)

        def put_b(row, value):
            put(row // B_PIECE, A_PIECE, value)

        for l in range(3):
            lanes = slice(l * 128, (l + 1) * 128)
            for k in range(2 * FPAD // 8):
                put_a(l * A_ROWS + k * 8, d_in_ref[k * 8 : k * 8 + 8, lanes])
            for k in range((A_ROWS - 2 * FPAD) // 8):
                put_a(l * A_ROWS + 2 * FPAD + k * 8, d_mid[k * 8 : k * 8 + 8, lanes])
            for k in range(B_ROWS // 8):
                put_b(l * B_ROWS + k * 8, d_mid[96 + k * 8 : 96 + k * 8 + 8, lanes])
        zeros = jnp.zeros((8, 128), f32)
        for row in range(3 * A_ROWS, OWNERS * A_PIECE, 8):
            put_a(row, zeros)
        vec = jnp.sum(vec_ref[...], axis=0, keepdims=True)
        for l in range(3):
            put_b(3 * B_ROWS + l * 8, jnp.broadcast_to(vec[:, l * 128 : (l + 1) * 128], (8, 128)))
        for row in range(3 * B_ROWS + 24, OWNERS * B_PIECE, 8):
            put_b(row, zeros)

    @pl.when(core == 0)
    def _():
        write((keep_ref, send_ref))

    @pl.when(core == 1)
    def _():
        write((send_ref, keep_ref))


def final_kernel(table_ref, field_ref, own_ref, recv_ref, out_ref, new_ref):
    from_slot = table_ref[0, 3]
    is_dyn = from_slot == 1
    keep_scale = jnp.where(is_dyn, 1.0, 0.0)
    new_scale = jnp.where(is_dyn, 0.5, 1.0)
    low_full = lane_ids((FPAD, COLS)) < COLS // 2

    def pair_body(i, carry):
        pair = own_ref[:, pl.ds(pl.multiple_of(i * COLS, COLS), COLS)].astype(f32)
        for side in range(2):
            r = 2 * i + side
            chunk = recv_ref[2 * r + from_slot].astype(f32)
            theirs = jnp.concatenate([swap_halves(chunk), chunk], axis=0)
            mine = pair if side == 0 else swap_halves(pair)
            tend = jnp.where(low_full, mine, theirs)
            tend = jnp.where(is_dyn, tend, swap_halves(tend))
            old = field_ref[table_ref[r, 0]]
            live = lane_ids((FPAD, COLS)) < table_ref[r, 1]
            new_ref[table_ref[r, 0]] = jnp.where(live, keep_scale * old + new_scale * tend, old)
        return carry

    lax.fori_loop(0, ROWS // 2, pair_body, 0, unroll=2)
    full, rest = chunks()

    def group(g, carry):
        value = jnp.swapaxes(new_ref[:, pl.ds(pl.multiple_of(g * 8, 8), 8), :], 0, 1)
        out_ref[pl.ds(pl.multiple_of(g * 128, 128), 128), :] = value.reshape(128, COLS)
        return carry

    lax.fori_loop(0, full, group, 0, unroll=2)
    value = jnp.swapaxes(new_ref[:, full * 8 : full * 8 + 8, :], 0, 1).reshape(128, COLS)
    out_ref[full * 128 :, :] = value[: rest * ROWS]


MID_A = 98
PERIOD = 23
OUT_AT = 3 * (HID - MID_A)


def gather_kernel(
    table_ref, mine_ref, x_other_ref, core_other_ref, far_ref, energy_ref, out_ref, all_ref, vec_ref
):
    is_dyn = table_ref[0, 3] == 1
    core = table_ref[0, 5]
    x = table_ref[0, 6]
    all_ref[2 * core + x] = mine_ref[...]
    all_ref[2 * core + 1 - x] = x_other_ref[...]
    all_ref[2 * (1 - core) + x] = core_other_ref[...]
    all_ref[2 * (1 - core) + 1 - x] = far_ref[...]

    def rows_at(row, count):
        quarter = OWNERS // 4 * A_PIECE
        parts = []
        while count:
            here = min(count, quarter - row % quarter)
            parts.append(all_ref[row // quarter, row % quarter : row % quarter + here, :])
            row, count = row + here, count - here
        return parts[0] if len(parts) == 1 else jnp.concatenate(parts, axis=0)

    @pl.when(is_dyn)
    def _():
        for l in range(3):
            for first, source, count in ((0, 0, FEAT), (FEAT, FPAD, FEAT), (2 * FEAT, 2 * FPAD, MID_A)):
                out_ref[pl.ds(3 * first + l, count, stride=3), :] = rows_at(
                    l * A_ROWS + source, count
                )

    @pl.when(jnp.logical_not(is_dyn))
    def _():
        skip = MID_A - 96
        for l in range(3):
            for m in range(B_ROWS // 8):
                value = rows_at((l * B_ROWS // 8 + m) * A_PIECE, 8)
                value = value[skip:] if m == 0 else value
                first = 0 if m == 0 else 8 * m - skip
                out_ref[pl.ds(3 * first + l, value.shape[0], stride=3), :] = value
        for l in range(3):
            value = rows_at((3 * B_ROWS // 8 + l) * A_PIECE, 8)
            value = jnp.concatenate([value] * 16, axis=0)
            vec_ref[l * 128 : (l + 1) * 128, :] = value.T
        vec_ref[HID:, :] = jnp.zeros((8, 128), f32)
        lane = lane_ids((HID // 8, 128))
        for k in range(PERIOD):
            h, start = 128 * k // OUT, 128 * k
            bound = OUT * (h + 1) - start
            value = vec_ref[pl.ds(h, HID // 8, stride=8), :]
            if bound < 128:
                after = vec_ref[pl.ds(h + 1, HID // 8, stride=8), :]
                value = jnp.where(lane < bound, value, after)
            out_ref[pl.ds(OUT_AT + k, HID // 8, stride=PERIOD), :] = value * energy_ref[k : k + 1, :]


def shape(dims, dtype):
    return jax.ShapeDtypeStruct(dims, dtype)


def swap(value, axis):
    return lax.ppermute(value, axis, [(0, 1), (1, 0)])


def on_device(columns, east_courant, north_courant, assign, block_cost, w_in, w_mid, w_out, energy):
    bands = lax.axis_size(LAT)
    lons = lax.axis_size(LON)
    is_physics = lax.axis_index("grp") == 1
    stored = columns.reshape(FLAT, COLS)

    n_copies = len(X_CUTS) - 1 + 4
    rim, corner, north_out, table = vmem_call(
        rim_kernel,
        [
            shape((128, COLS), bf16),
            shape((128, COLS), bf16),
            shape((2 * FPAD, COLS), bf16),
            shape((ROWS, COLS), jnp.int32),
        ],
        [
            pltpu.VMEM((FLAT, COLS), f32),
            pltpu.VMEM((ROWS, COLS), f32),
            pltpu.VMEM((ROWS, COLS), f32),
            pltpu.VMEM((ROWS, ROWS), jnp.int32),
            pltpu.VMEM((ROWS, ROWS), jnp.int32),
            pltpu.SemaphoreType.DMA((n_copies,)),
        ],
        "hhhhh",
        10**8,
        3 * 10**6,
        "rim",
        ALL_VMEM,
    )(stored, east_courant, north_courant, assign, block_cost)
    from_west = lax.ppermute(rim, LON, [(i, (i + 1) % lons) for i in range(lons)])
    from_south = lax.ppermute(north_out, LAT, [(i, i + 1) for i in range(bands - 1)])
    from_corner = lax.ppermute(
        corner,
        LAT + LON,
        [(b * lons + i, (b + 1) * lons + (i + 1) % lons) for b in range(bands - 1) for i in range(lons)],
    )

    def halves(a, b, axis):
        first = jnp.where(is_physics, b, a)
        second = jnp.where(is_physics, a, b)
        pad = [(0, 0), (0, 0)]
        pad[axis] = (0, FPAD - FEAT)
        return jnp.concatenate([jnp.pad(first, pad), jnp.pad(second, pad)], axis=axis)

    w_in_t = w_in.T
    w_one = halves(w_in_t[:, :FEAT], w_in_t[:, FEAT:], 1)
    w_out_t = w_out.T
    w_three = halves(w_out_t[:FEAT], w_out_t[OUT - FEAT :], 0)
    gain = jnp.sum(w_out.astype(f32) * energy[None, :], axis=1, keepdims=True)

    field, own, send = vmem_call(
        transport_kernel,
        [
            shape((ROWS, FPAD, COLS), f32),
            shape((ROWS // 2, FPAD, COLS), bf16),
            shape((2 * ROWS, PACK, COLS), bf16),
        ],
        [
            pltpu.VMEM((GROUPS * 128, COLS), f32),
            pltpu.VMEM((ROWS, FPAD, COLS), f32),
            pltpu.VMEM((128, COLS), f32),
            pltpu.VMEM((ROWS, 8, COLS), f32),
            pltpu.VMEM((2 * FPAD, COLS), f32),
            pltpu.VMEM((ROWS // 2, FPAD, COLS), bf16),
            pltpu.VMEM((ROWS, PACK, COLS), bf16),
            pltpu.SemaphoreType.DMA((1 + ROWS + ROWS // 2 + 2 * (len(X_CUTS) - 1),)),
        ],
        "shvvvvv",
        10**8,
        6 * 10**6,
        "transport",
        ALL_VMEM,
        "hhh",
    )(table, stored, east_courant, north_courant, from_west, from_south, from_corner)
    recv = lax.all_to_all(send, LON + ("grp",), 0, 0, tiled=True)
    inputs, hidden, g_two, slope, own_out, send_back, vec = vmem_call(
        forward_kernel,
        [
            shape((2 * FPAD, MINE), bf16),
            shape((HID, MINE), bf16),
            shape((HID, MINE), bf16),
            shape((HID, MINE), f32),
            shape((FPAD, MINE), bf16),
            shape((2 * ROWS, PACK, COLS), bf16),
            shape((16, HID), f32),
        ],
        [],
        "svvvvvv",
        2 * MINE * HID * (4 * FPAD + HID),
        8 * 10**6,
        "forward",
        16,
    )(table, own, recv, w_one, w_mid.T, w_three, gain)
    back = lax.all_to_all(send_back, LON + ("grp",), 0, 0, tiled=True)
    keep, other = vmem_call(
        backward_kernel,
        [shape((OWNERS // 2, PIECE, 128), f32)] * 2,
        [pltpu.VMEM((HID, MINE), bf16), pltpu.VMEM((2 * FPAD, HID), f32)],
        "svvvvvv",
        2 * MINE * HID * (2 * FPAD + 2 * HID),
        6 * 10**6,
        "backward",
        16,
    )(table, inputs, hidden, g_two, slope, w_mid, vec)

    grad = keep + swap(other, "core")
    for axis in ("zc", "zb"):
        pieces = grad.shape[0] // 2
        at = lax.axis_index(axis)
        other = lax.dynamic_slice_in_dim(grad, (1 - at) * pieces, pieces)
        keep = lax.dynamic_slice_in_dim(grad, at * pieces, pieces)
        other = swap(other.astype(bf16), axis)
        if axis == "zb":
            other, back = lax.optimization_barrier((other, back))
        grad = keep + other.astype(f32)
    pieces_b = jnp.pad(grad[:, A_PIECE:], ((0, 0), (0, A_PIECE - B_PIECE), (0, 0)))
    pieces = jnp.stack([grad[:, :A_PIECE], pieces_b], axis=1).reshape(-1, A_PIECE, 128)
    piece = jnp.sum(lax.all_to_all(pieces, ("za", "y", "x", "grp"), 0, 0, tiled=True), axis=0)
    ring = LAT + ("y",)
    members = bands * lax.axis_size("y")
    piece = lax.all_to_all(
        jnp.broadcast_to(piece[None], (members,) + piece.shape), ring, 0, 0, tiled=True
    )
    new = vmem_call(
        final_kernel,
        [shape((FLAT, COLS), f32)],
        [pltpu.VMEM((ROWS, FPAD, COLS), f32)],
        "svvv",
        10**7,
        6 * 10**6,
        "final",
        16,
    )(table, field, own_out, back)[0]
    core_other = swap(piece, "core")
    x_other = swap(piece, "x")
    x_other, new = lax.optimization_barrier((x_other, new))
    far = swap(x_other, "core")
    energy_rows = jnp.tile(energy, 8).reshape(PERIOD, 128)
    quarter = (OWNERS // 4 * A_PIECE, 128)
    grad_half = vmem_call(
        gather_kernel,
        [shape((3 * (2 * FEAT + MID_A), 128), f32)],
        [pltpu.VMEM((4,) + quarter, f32), pltpu.VMEM((HID + 8, 128), f32)],
        "svvvvv",
        10**7,
        2 * 10**6,
        "gather",
        16,
    )(table, *(value.reshape(quarter) for value in (piece, x_other, core_other, far)), energy_rows)[0]
    return new.reshape(columns.shape), grad_half.reshape(-1)


def solution(mesh):
    lat, lon, grp = mesh.devices.shape
    split = Mesh(mesh.devices.reshape(lat // 4, 2, 2, lon // 4, 2, 2, grp), LAT + LON + ("grp",))
    grid = P(LAT, LON)
    columns = P("grp", None, LAT, LON)
    return jax.shard_map(
        on_device,
        mesh=split,
        in_specs=(columns, grid, grid, P(), P(), P(), P(), P(), P()),
        out_specs=(columns, P("grp")),
        check_vma=False,
    )
```
